128 devices in a mesh: dp: 32 (over x, z, core), outer: 4 (over y).
Axes of the slice: x: 4, y: 4, z: 4, core: 2. Of those that a mesh axis runs over, the one named last changes fastest.
Arguments:
- tokens_in: bfloat16 [49152, 960], P(('dp', 'outer')), may hold values from -16 to 16
- segment_ids: int32 [49152], P(('dp', 'outer')), may hold values from 0 to 4, as said below
- norm_in: bfloat16 [960], P('dp'), may hold values from 0.099609375 to 1.8984375
- w_query: bfloat16 [960, 960], P('dp'), may hold values from -0.1875 to 0.1875
- w_key: bfloat16 [960, 320], P('dp'), may hold values from -0.1875 to 0.1875
- w_value: bfloat16 [960, 320], P('dp'), may hold values from -0.1875 to 0.1875
- w_out: bfloat16 [960, 960], P('dp'), may hold values from -0.75 to 0.75
- norm_mid: bfloat16 [960], P('dp'), may hold values from 0.099609375 to 1.8984375
- w_gate: bfloat16 [960, 2560], P('dp'), may hold values from -0.1875 to 0.1875
- w_up: bfloat16 [960, 2560], P('dp'), may hold values from -0.1875 to 0.1875
- w_down: bfloat16 [2560, 960], P('dp'), may hold values from -0.125 to 0.125
- out_cotangent: bfloat16 [49152, 960], P(('dp', 'outer')), may hold values from -6 to 6
Outputs:
- layer_out: bfloat16 [49152, 960], P(('dp', 'outer'))
- grad_input: bfloat16 [49152, 960], P(('dp', 'outer'))
- grad_norm_in: float32 [960], P('dp')
- grad_query: float32 [960, 960], P('dp')
- grad_key: float32 [960, 320], P('dp')
- grad_value: float32 [960, 320], P('dp')
- grad_out: float32 [960, 960], P('dp')
- grad_norm_mid: float32 [960], P('dp')
- grad_gate: float32 [960, 2560], P('dp')
- grad_up: float32 [960, 2560], P('dp')
- grad_down: float32 [2560, 960], P('dp')
The draws below stay inside these ranges and needn't reach their ends.
Inputs may be any that keep to these rules, and one draw needn't show every extreme that they name: `segment_ids`: within each aligned block of 128 slots the ids never fall and start live at slot 0; 4 marks padding, which fills the end of a block; every block has half of its slots or more live, some blocks are full and some half padding.
All inputs are finite; a program needn't handle non-finite values.
Results may differ from the reference program's by a relative error of at most 0.028.
Values may be sent and summed in bfloat16 or wider, within the bound.
No kernel may reach another device: no remote copies, remote signals or barrier semaphores. Data moves between devices by JAX's collectives and lax.ppermute only.
A program may use at most 256 MiB of HBM per device.

```python
import math
import jax
import jax.numpy as jnp
from jax import lax

D = 960
FF = 2560
HEADS = 15
KV_HEADS = 5
HEAD_DIM = 64
MB_ROWS = 128
DOCS = 4
TOKENS = 49152


def draw_segment_ids(key, part):
    key = jax.random.fold_in(key, 11)
    used_key, cut_key = jax.random.split(key)
    block_count = TOKENS // MB_ROWS
    used_slots = jax.random.randint(used_key, (block_count,), MB_ROWS // 2, MB_ROWS + 1)
    used_slots = used_slots.at[0].set(MB_ROWS).at[1].set(MB_ROWS // 2)
    cut_points = jax.random.randint(cut_key, (block_count, DOCS - 1), 1, MB_ROWS)
    index = jnp.arange(MB_ROWS, dtype=jnp.int32)
    numbers = jnp.sum((index[None, :, None] >= cut_points[:, None, :]).astype(jnp.int32), axis=2)
    numbers = jnp.where(index[None, :] < used_slots[:, None], numbers, DOCS)
    return numbers.reshape(TOKENS).astype(jnp.int32)


def spiked(entries, own_key, source, target, blocks, factor):
    owner, partner = [(jnp.arange(entries.shape[dim]) // (entries.shape[dim] // blocks)).reshape([-1 if axis == dim else 1 for axis in range(entries.ndim)]) for dim in (source, target)]
    chosen = jax.random.permutation(own_key, blocks)[partner]
    strong = (owner == chosen) | (owner == (partner + blocks // 2) % blocks)
    return jnp.where(strong, factor * entries, entries)


def block_scale(own_key, shape, shards, smallest, high):
    def one(position, parts):
        heights = jax.random.uniform(jax.random.fold_in(jax.random.fold_in(own_key, 6), position), (parts,), jnp.float32, smallest / len(shards), high / len(shards))
        return jnp.repeat(jnp.exp(heights), shape[position] // parts).reshape((-1,) + (1,) * (len(shape) - position - 1))

    gain = one(*shards[0])
    for cut in shards[1:]:
        gain = gain * one(*cut)
    return gain


def centred(rng, shape, spread, reach, cuts=(), held_as=jnp.bfloat16):
    array = jax.random.normal(rng, shape, jnp.float32) * spread
    if len(cuts) > 0:
        array = block_scale(rng, shape, cuts, -0.22, 0.18) * array
    return jnp.clip(array, min=-reach, max=reach).astype(held_as)


def gaussian_with(own_key, extent, width, most, cuts, heavy, kind=jnp.bfloat16):
    array = width * jax.random.normal(own_key, extent, jnp.float32)
    if cuts:
        array = array * block_scale(own_key, extent, cuts, -0.22, 0.18)
    return jnp.clip(spiked(array, jax.random.fold_in(own_key, 3), *heavy), -most, most).astype(kind)


def setup_inputs(seed: int = 0) -> dict:
    key_list = jax.random.split(jax.random.key(seed), 13)
    tokens_in = gaussian_with(key_list[0], (TOKENS, D), 1.0, 16.0, ((0, 128),), (0, 1, 64, 4.0))
    segment_ids = draw_segment_ids(jax.random.fold_in(key_list[12], 71), 0)
    norm_in = jnp.clip(1.0 + 0.18 * jax.random.normal(key_list[2], (D,), jnp.float32), 0.099609375, 1.8984375).astype(jnp.bfloat16)
    w_query = centred(key_list[3], (D, HEADS * HEAD_DIM), D ** -0.5, 0.1875, ((0, 32),))
    w_key = centred(key_list[4], (D, KV_HEADS * HEAD_DIM), D ** -0.5, 0.1875, ((0, 32),))
    w_value = centred(key_list[5], (D, KV_HEADS * HEAD_DIM), D ** -0.5, 0.1875, ((0, 32),))
    w_out = centred(key_list[6], (HEADS * HEAD_DIM, D), (D // 16) ** -0.5, 0.75, ((0, 32),))
    norm_mid = jnp.clip(1.0 + 0.18 * jax.random.normal(key_list[7], (D,), jnp.float32), 0.099609375, 1.8984375).astype(jnp.bfloat16)
    w_gate = centred(key_list[8], (D, FF), D ** -0.5, 0.1875, ((0, 32),))
    w_up = centred(key_list[9], (D, FF), D ** -0.5, 0.1875, ((0, 32),))
    w_down = centred(key_list[10], (FF, D), FF ** -0.5, 0.125, ((0, 32),))
    out_cotangent = centred(key_list[11], (TOKENS, D), 1.0, 6.0, ((0, 128),))
    return dict(tokens_in=tokens_in, segment_ids=segment_ids, norm_in=norm_in, w_query=w_query, w_key=w_key, w_value=w_value, w_out=w_out, norm_mid=norm_mid, w_gate=w_gate, w_up=w_up, w_down=w_down, out_cotangent=out_cotangent)


@jax.custom_vjp
def low(v):
    return lax.optimization_barrier(v.astype(jnp.bfloat16)).astype(jnp.float32)

@jax.custom_vjp
def low_back(v):
    return v

def low_keep(v):
    return (low(v), None)

def low_pass(kept, grad):
    return (grad,)

def back_keep(v):
    return (v, None)

def back_low(kept, grad):
    return (low(grad),)
low.defvjp(low_keep, low_pass)
low_back.defvjp(back_keep, back_low)
EPSILON = 1e-05
ROPE_BASE = 100000.0
HIGHEST = lax.Precision.HIGHEST

def matmul(left, right):
    return jnp.dot(left, right, precision=HIGHEST)

def rms_scale(values):
    return lax.rsqrt(lax.optimization_barrier(jnp.mean(values * values, axis=-1, keepdims=True)) + EPSILON)

def rotate(values, cosine, sine):
    middle = values.shape[-1] // 2
    first_half = values[..., :middle]
    second_half = values[..., middle:]
    return jnp.concatenate([first_half * cosine - second_half * sine, second_half * cosine + first_half * sine], axis=-1)

def rope_tables(segment):
    span_size = segment.shape[-1]
    index = jnp.arange(span_size, dtype=jnp.int32)
    change = jnp.concatenate([jnp.ones(segment.shape[:-1] + (1,), dtype=bool), segment[..., 1:] != segment[..., :-1]], axis=-1)
    starts = lax.cummax(jnp.where(change, index, 0), axis=segment.ndim - 1)
    offset = (index - starts).astype(jnp.float32)
    inverse_freq = jnp.exp(jnp.arange(HEAD_DIM // 2, dtype=jnp.float32) * (-2.0 * math.log(ROPE_BASE) / HEAD_DIM))
    angles = offset[..., None] * inverse_freq
    return (jnp.cos(angles)[..., None, :], jnp.sin(angles)[..., None, :])

def allowed_pairs(segment):
    index = jnp.arange(segment.shape[-1], dtype=jnp.int32)
    same_doc = segment[..., :, None] == segment[..., None, :]
    return same_doc & (index[:, None] >= index[None, :])

def forward(params, inputs, cosine, sine, allowed, live_rows):
    norm_in, w_query, w_key, w_value, w_out, norm_mid, w_gate, w_up, w_down = params
    groups, row_count, width_all = inputs.shape
    share = HEADS // KV_HEADS
    flat = inputs.reshape(groups * row_count, width_all)
    normed_in = low(flat * rms_scale(flat) * norm_in)
    query_raw = low_back(matmul(normed_in, w_query)).reshape(groups, row_count, HEADS, HEAD_DIM)
    key_raw = low_back(matmul(normed_in, w_key)).reshape(groups, row_count, KV_HEADS, HEAD_DIM)
    value_low = low(low_back(matmul(normed_in, w_value))).reshape(groups, row_count, KV_HEADS, HEAD_DIM)
    query_low = low(rotate(query_raw, cosine, sine)).reshape(groups, row_count, KV_HEADS, share, HEAD_DIM)
    key_low = low(rotate(key_raw, cosine, sine))
    scores = low_back(jnp.einsum('grksd,gtkd->gksrt', query_low, key_low, precision=HIGHEST) * HEAD_DIM ** (-0.5))
    scores = jnp.where(allowed[:, None, None], scores, -1e+30)
    probs = jnp.exp(scores - lax.optimization_barrier(jnp.max(scores, axis=-1, keepdims=True)))
    probs = probs / lax.optimization_barrier(jnp.sum(probs, axis=-1, keepdims=True))
    mixed = jnp.einsum('gksrt,gtkd->grksd', low(probs), value_low, precision=HIGHEST)
    mixed = low(low_back(mixed.reshape(groups * row_count, HEADS * HEAD_DIM)))
    after_attn = flat + low_back(matmul(mixed, w_out))
    normed_mid = low(after_attn * rms_scale(after_attn) * norm_mid)
    gate_pre = low_back(matmul(normed_mid, w_gate))
    up_pre = low_back(matmul(normed_mid, w_up))
    hidden = low(jax.nn.silu(gate_pre) * up_pre)
    result = after_attn + low_back(matmul(hidden, w_down))
    return (result * live_rows).reshape(groups, row_count, width_all)

def reference(tokens_in, segment_ids, norm_in, w_query, w_key, w_value, w_out, norm_mid, w_gate, w_up, w_down, out_cotangent):
    params = tuple((p.astype(jnp.float32) for p in (norm_in, w_query, w_key, w_value, w_out, norm_mid, w_gate, w_up, w_down)))
    group_size = 8
    width_all = tokens_in.shape[1]
    step_count = tokens_in.shape[0] // (MB_ROWS * group_size)
    inputs_all = tokens_in.astype(jnp.float32).reshape(step_count, group_size, MB_ROWS, width_all)
    segments_all = segment_ids.reshape(step_count, group_size, MB_ROWS)
    cotangent_all = out_cotangent.astype(jnp.float32).reshape(step_count, group_size, MB_ROWS, width_all)

    def one_step(totals, items):
        inputs, segment, cotangent = items
        cosine, sine = rope_tables(segment)
        allowed = allowed_pairs(segment)
        live_rows = (segment < DOCS).astype(jnp.float32).reshape(group_size * MB_ROWS, 1)

        def layer(weights, values):
            return forward(weights, values, cosine, sine, allowed, live_rows)
        result, pullback = jax.vjp(layer, params, inputs)
        grad_params, grad_values = pullback(cotangent)
        totals = jax.tree.map(jnp.add, totals, grad_params)
        return (totals, (result.astype(jnp.bfloat16), grad_values.astype(jnp.bfloat16)))
    zeros_init = tuple((jnp.zeros(p.shape, jnp.float32) for p in params))
    totals, (results, grads_in) = lax.scan(one_step, zeros_init, (inputs_all, segments_all, cotangent_all))
    return (results.reshape(-1, width_all), grads_in.reshape(-1, width_all)) + tuple(totals)
```

```python
import math

import jax
import jax.numpy as jnp
from jax import lax
from jax.experimental import pallas as pl
from jax.experimental.pallas import tpu as pltpu
from jax.sharding import PartitionSpec as P

HEADS = 15
KV_HEADS = 5
SHARE = HEADS // KV_HEADS
HEAD_DIM = 64
MB = 128
DOCS = 4
D = 960
FF = 2560
QKV = 1600
ROT = 1280
NX = 4
NZ = 4
PIECES = 32
ROWS = 30
PAD = 32
DP = PIECES * PAD
HALF = DP // 2
DOWN = FF // PIECES

EPSILON = 1e-05
ROPE_BASE = 100000.0
BF = jnp.bfloat16
F32 = jnp.float32


def dot(a, b):
    return jnp.dot(a, b, preferred_element_type=F32)


def dot_nt(a, b):
    return lax.dot_general(a, b, (((1,), (1,)), ((), ())), preferred_element_type=F32)


def dot_tn(a, b):
    return lax.dot_general(a, b, (((0,), (0,)), ((), ())), preferred_element_type=F32)


def rms_scale(v):
    return lax.rsqrt(jnp.mean(v * v, axis=-1, keepdims=True) + EPSILON)


def swap_halves(v):
    n = v.shape[1]
    lane = lax.broadcasted_iota(jnp.int32, v.shape, 1)
    return jnp.where(lane % HEAD_DIM < HEAD_DIM // 2, pltpu.roll(v, n - 32, 1), pltpu.roll(v, 32, 1))


def attn_forward(qkv_ref, cos_ref, sin_ref, segc_ref, segr_ref, rot_ref, out_ref, prob_ref):
    blocks = qkv_ref.shape[0] // MB
    for b in range(blocks):
        rows = slice(b * MB, (b + 1) * MB)
        raw = qkv_ref[rows, :ROT]
        cos = jnp.concatenate([cos_ref[rows, :]] * (ROT // 128), axis=1)
        sin = jnp.concatenate([sin_ref[rows, :]] * (ROT // 128), axis=1)
        rot_ref[rows, :ROT] = (raw * cos + swap_halves(raw) * sin).astype(BF)
        rot_ref[rows, ROT:] = qkv_ref[rows, ROT:].astype(BF)
        r = lax.broadcasted_iota(jnp.int32, (MB, MB), 0)
        t = lax.broadcasted_iota(jnp.int32, (MB, MB), 1)
        allowed = (segc_ref[rows, :] == segr_ref[b : b + 1, :]) & (r >= t)
        allowed = jnp.concatenate([allowed] * SHARE, axis=0)
        for g in range(KV_HEADS):
            q = jnp.concatenate(
                [rot_ref[rows, (g * SHARE + j) * HEAD_DIM : (g * SHARE + j + 1) * HEAD_DIM] for j in range(SHARE)],
                axis=0,
            )
            k = rot_ref[rows, D + g * HEAD_DIM : D + (g + 1) * HEAD_DIM]
            v = rot_ref[rows, ROT + g * HEAD_DIM : ROT + (g + 1) * HEAD_DIM]
            s = jnp.where(allowed, dot_nt(q, k) * HEAD_DIM ** (-0.5), -1e30)
            e = jnp.exp(s - jnp.max(s, axis=-1, keepdims=True))
            p = e / jnp.sum(e, axis=-1, keepdims=True)
            at = (b * KV_HEADS + g) * SHARE * MB
            prob_ref[at : at + SHARE * MB, :] = p
            o = dot(p.astype(BF), v).astype(BF)
            for j in range(SHARE):
                h = g * SHARE + j
                out_ref[rows, h * HEAD_DIM : (h + 1) * HEAD_DIM] = o[j * MB : (j + 1) * MB, :]


def attn_backward(do_ref, rot_ref, prob_ref, cos_ref, sin_ref, dqkv_ref, work_ref):
    blocks = do_ref.shape[0] // MB
    scale = HEAD_DIM ** (-0.5)
    for b in range(blocks):
        rows = slice(b * MB, (b + 1) * MB)
        for g in range(KV_HEADS):
            heads = [slice((g * SHARE + j) * HEAD_DIM, (g * SHARE + j + 1) * HEAD_DIM) for j in range(SHARE)]
            q = jnp.concatenate([rot_ref[rows, h] for h in heads], axis=0)
            do = jnp.concatenate([do_ref[rows, h] for h in heads], axis=0)
            k = rot_ref[rows, D + g * HEAD_DIM : D + (g + 1) * HEAD_DIM]
            v = rot_ref[rows, ROT + g * HEAD_DIM : ROT + (g + 1) * HEAD_DIM]
            at = (b * KV_HEADS + g) * SHARE * MB
            p = prob_ref[at : at + SHARE * MB, :]
            dp = dot_nt(do, v)
            dv = dot_tn(p.astype(BF), do)
            delta = jnp.sum(p * dp, axis=-1, keepdims=True)
            ds = (p * (dp - delta)).astype(BF)
            dq = dot(ds, k) * scale
            dk = dot_tn(ds, q) * scale
            for j in range(SHARE):
                work_ref[:, heads[j]] = dq[j * MB : (j + 1) * MB, :]
            work_ref[:, D + g * HEAD_DIM : D + (g + 1) * HEAD_DIM] = dk
            dqkv_ref[rows, ROT + g * HEAD_DIM : ROT + (g + 1) * HEAD_DIM] = dv.astype(BF)
        cos = jnp.concatenate([cos_ref[rows, :]] * (ROT // 128), axis=1)
        sin = jnp.concatenate([sin_ref[rows, :]] * (ROT // 128), axis=1)
        w = work_ref[...]
        dqkv_ref[rows, :ROT] = (w * cos - swap_halves(w) * sin).astype(BF)


def rope_tables(segment):
    n = segment.shape[0]
    seg = segment.reshape(n // MB, MB)
    index = lax.broadcasted_iota(jnp.int32, (n // MB, MB, MB), 2)
    same = seg[:, :, None] == seg[:, None, :]
    first = jnp.min(jnp.where(same, index, MB), axis=2)
    place = (jnp.arange(MB, dtype=jnp.int32)[None, :] - first).astype(F32).reshape(n, 1)
    lane = jnp.arange(128, dtype=jnp.int32)
    freq = jnp.exp((lane % 32).astype(F32) * (-2.0 * math.log(ROPE_BASE) / HEAD_DIM))
    angles = place * freq[None, :]
    sign = jnp.where(lane % 64 < 32, -1.0, 1.0)[None, :]
    return jnp.cos(angles), jnp.sin(angles) * sign


def padding_matrix(x, z, c):
    i = lax.broadcasted_iota(jnp.int32, (D, HALF), 0)
    j = lax.broadcasted_iota(jnp.int32, (D, HALF), 1)
    j_x = (x + j // (NZ * PAD)) % NX
    j_z = (z + j // PAD % NZ) % NZ
    j_r = j % PAD
    row = ((j_x * NZ + j_z) * 2 + c) * ROWS + j_r
    return ((i == row) & (j_r < ROWS)).astype(BF)


def natural_matrix():
    i = lax.broadcasted_iota(jnp.int32, (D, DP), 0)
    j = lax.broadcasted_iota(jnp.int32, (D, DP), 1)
    return ((i // ROWS) * PAD + i % ROWS == j).astype(BF)


def vmem_call(kernel, out_shape, scratch=()):
    return pl.pallas_call(
        kernel,
        out_shape=out_shape,
        scratch_shapes=list(scratch),
        compiler_params=pltpu.CompilerParams(vmem_limit_bytes=48 * 1024 * 1024),
    )


def place_of(x, z, c):
    return (x * NZ + z) * 2 + c


def shift(v, axis, s):
    perm = []
    for x in range(NX):
        for z in range(NZ):
            for c in range(2):
                to = {
                    "x": ((x + s) % NX, z, c),
                    "z": (x, (z + s) % NZ, c),
                    "c": (x, z, 1 - c),
                }[axis]
                perm.append((place_of(x, z, c), place_of(*to)))
    return lax.ppermute(v, "dp", perm)


def ring_gather(s, axis, cut):
    a = shift(s, axis, 1)
    b = shift(s, axis, -1)
    a2 = shift(a[:cut], axis, 1)
    b2 = shift(b[cut:], axis, -1)
    return [s, b, jnp.concatenate([a2, b2], axis=0), a]


def gather_half(s, first):
    rows, n = s.shape
    second = "z" if first == "x" else "x"
    one = jnp.stack(ring_gather(s, first, rows // 32 * 16), axis=0)
    two = ring_gather(one, second, 2)
    mine = jnp.stack(two, axis=1 if first == "x" else 0)
    return mine, shift(mine, "c", 1)


def ring_sum(take, axis, cut):
    two = take(2)
    from_left = shift(two[:cut], axis, 1)
    from_right = shift(two[cut:], axis, -1)
    one = take(1)
    three = take(3)
    one = jnp.concatenate([one[:cut] + from_left, one[cut:]], axis=0)
    three = jnp.concatenate([three[:cut], three[cut:] + from_right], axis=0)
    a = shift(one, axis, 1)
    b = shift(three, axis, -1)
    return (take(0).astype(F32) + a.astype(F32) + b.astype(F32)).astype(BF)


def reduce_gradient(mine, other, rows, first):
    n = mine.shape[-1]
    h = (mine.astype(F32) + shift(other, "c", 1).astype(F32)).astype(BF).reshape(NX, NZ, rows, n)
    if first == "x":
        h = ring_sum(lambda k: h[k], "x", 2)
        second = "z"
    else:
        h = ring_sum(lambda k: h[:, k], "z", 2)
        second = "x"
    h = ring_sum(lambda k: h[k], second, rows // 32 * 16)
    h = h + lax.ppermute(h, "outer", [(0, 1), (1, 0), (2, 3), (3, 2)])
    t = lax.ppermute(h, "outer", [(0, 3), (3, 0), (1, 2), (2, 1)])
    return h.astype(F32) + t.astype(F32)


def mlp(pos, h2_ref, e_ref, x1_ref, live_ref, wg_ref, wu_ref, dm_ref, do_ref,
        out_ref, dgate_ref, dup_ref, gm_ref, go_ref, dh_ref, acc_ref, w_ref, g_ref):
    step = pl.program_id(0)
    z, c = pos[1], pos[2]

    def at(kz, core):
        return pl.ds(pl.multiple_of(lax.rem(z + kz, NZ) * (2 * DOWN) + core * DOWN, 16), DOWN)

    for kz in range(NZ):
        w_ref[at(kz, c), :] = dm_ref[0, kz]
        w_ref[at(kz, 1 - c), :] = do_ref[0, kz]
    h2 = h2_ref[...]
    e = e_ref[...]
    gate = dot(h2, wg_ref[...])
    up = dot(h2, wu_ref[...])
    sig = jax.nn.sigmoid(gate)
    silu = gate * sig
    hidden = (silu * up).astype(BF)
    g_ref[...] = dot_tn(hidden, e)
    for kz in range(NZ):
        gm_ref[0, kz] = g_ref[at(kz, c), :].astype(BF)
        go_ref[0, kz] = g_ref[at(kz, 1 - c), :].astype(BF)
    d_hidden = dot_nt(e, w_ref[...])
    d_gate = (d_hidden * up * sig * (1.0 + gate * (1.0 - sig))).astype(BF)
    d_up = (d_hidden * silu).astype(BF)
    dgate_ref[...] = d_gate
    dup_ref[...] = d_up
    dh = dot_nt(d_gate, wg_ref[...]) + dot_nt(d_up, wu_ref[...])
    y = dot(hidden, w_ref[...])

    @pl.when(step == 0)
    def _():
        dh_ref[...] = dh
        acc_ref[...] = x1_ref[...] + y

    @pl.when(step > 0)
    def _():
        dh_ref[...] += dh
        acc_ref[...] += y

    @pl.when(step == NX - 1)
    def _():
        out_ref[...] = (acc_ref[...] * live_ref[...]).astype(BF)


def mlp_call(pos, h2, e, x1, live, gate_up, down_mine, down_other):
    n = h2.shape[0]
    tile = FF // NX

    def whole(a):
        return pl.BlockSpec(a.shape, lambda k, pos: (0,) * a.ndim)

    def shard(off):
        return pl.BlockSpec((DP, tile), lambda k, pos: (0, off + lax.rem(pos[0] + k, NX)))

    down = pl.BlockSpec((1, NZ, DOWN, D), lambda k, pos: (k, 0, 0, 0))
    cols = pl.BlockSpec((n, tile), lambda k, pos: (0, lax.rem(pos[0] + k, NX)))
    return pl.pallas_call(
        mlp,
        out_shape=(
            jax.ShapeDtypeStruct((n, D), BF),
            jax.ShapeDtypeStruct((n, FF), BF),
            jax.ShapeDtypeStruct((n, FF), BF),
            jax.ShapeDtypeStruct((NX, NZ, DOWN, D), BF),
            jax.ShapeDtypeStruct((NX, NZ, DOWN, D), BF),
            jax.ShapeDtypeStruct((n, DP), F32),
        ),
        grid_spec=pltpu.PrefetchScalarGridSpec(
            num_scalar_prefetch=1,
            grid=(NX,),
            in_specs=[whole(h2), whole(e), whole(x1), whole(live), shard(0), shard(NX), down, down],
            out_specs=(
                pl.BlockSpec((n, D), lambda k, pos: (0, 0)),
                cols,
                cols,
                down,
                down,
                pl.BlockSpec((n, DP), lambda k, pos: (0, 0)),
            ),
            scratch_shapes=[
                pltpu.VMEM((n, D), F32),
                pltpu.VMEM((tile, D), BF),
                pltpu.VMEM((tile, D), F32),
            ],
        ),
        compiler_params=pltpu.CompilerParams(
            vmem_limit_bytes=48 * 1024 * 1024, dimension_semantics=("arbitrary",)
        ),
        cost_estimate=pl.CostEstimate(flops=14 * n * D * FF, bytes_accessed=30 * 1024 * 1024, transcendentals=n * FF),
    )(pos, h2, e, x1, live, gate_up, gate_up, down_mine, down_other)


def pad_rows(w):
    return jnp.pad(w, ((0, PAD - ROWS), (0, 0)))


def local(
    tokens_in,
    segment_ids,
    norm_in,
    w_query,
    w_key,
    w_value,
    w_out,
    norm_mid,
    w_gate,
    w_up,
    w_down,
    out_cotangent,
):
    n = tokens_in.shape[0]
    me = lax.axis_index("dp")
    c_at = me % 2
    z_at = (me // 2) % NZ
    x_at = me // (2 * NZ)
    pos = jnp.stack([x_at, z_at, c_at]).astype(jnp.int32)
    gain_in = norm_in.astype(F32)[:, None]
    gain_mid = norm_mid.astype(F32)[:, None]
    s_qkv = jnp.concatenate([w_query, w_key, w_value], axis=1).astype(F32)
    s_gu = jnp.concatenate([w_gate, w_up], axis=1).astype(F32)
    gate_up = lax.all_gather(pad_rows((s_gu * gain_mid).astype(BF)), "dp", axis=0, tiled=True)
    qkv_m, qkv_o = gather_half(pad_rows((s_qkv * gain_in).astype(BF)), "x")
    out_m, out_o = gather_half(pad_rows(w_out), "z")
    down_m, down_o = gather_half(w_down, "z")
    qkv_m, qkv_o = qkv_m.reshape(HALF, QKV), qkv_o.reshape(HALF, QKV)
    out_m, out_o = out_m.reshape(HALF, D), out_o.reshape(HALF, D)

    pad_m = padding_matrix(x_at, z_at, c_at)
    pad_o = padding_matrix(x_at, z_at, 1 - c_at)
    natural = natural_matrix()
    cos, sin = rope_tables(segment_ids)
    live = (segment_ids < DOCS).astype(F32)[:, None]
    x = tokens_in.astype(F32)

    s1 = rms_scale(x)
    h1 = (x * s1).astype(BF)
    h1_m, h1_o = dot(h1, pad_m).astype(BF), dot(h1, pad_o).astype(BF)
    qkv = dot(h1_m, qkv_m) + dot(h1_o, qkv_o)
    rot, mixed, probs = vmem_call(
        attn_forward,
        (
            jax.ShapeDtypeStruct((n, QKV), BF),
            jax.ShapeDtypeStruct((n, D), BF),
            jax.ShapeDtypeStruct((n * HEADS, MB), F32),
        ),
    )(qkv, cos, sin, segment_ids[:, None], segment_ids.reshape(n // MB, MB))
    mixed_m, mixed_o = dot(mixed, pad_m).astype(BF), dot(mixed, pad_o).astype(BF)
    x1 = x + dot(mixed_m, out_m) + dot(mixed_o, out_o)
    s2 = rms_scale(x1)
    h2 = (x1 * s2).astype(BF)
    h2_m, h2_o = dot(h2, pad_m).astype(BF), dot(h2, pad_o).astype(BF)
    e_low = (out_cotangent.astype(F32) * live).astype(BF)
    layer_out, d_gate, d_up, gd_m, gd_o, dh2 = mlp_call(
        pos, dot(h2, natural).astype(BF), e_low, x1, live, gate_up, down_m, down_o
    )
    g_down = reduce_gradient(gd_m, gd_o, DOWN, "x")
    d_gu = jnp.concatenate([d_gate, d_up], axis=1)
    g_gu = reduce_gradient(dot_tn(h2_m, d_gu), dot_tn(h2_o, d_gu).astype(BF), PAD, "z")[:ROWS]

    def split(v):
        high = v.astype(BF)
        return high, (v - high.astype(F32)).astype(BF)

    high, low = split(dh2)
    dn = dot_nt(high, natural) + dot_nt(low, natural)
    d_x1 = e_low.astype(F32) + s2 * dn - x1 * s2**3 * jnp.mean(dn * x1, axis=-1, keepdims=True)
    d_a = d_x1.astype(BF)
    d_o = dot_nt(dot_nt(d_a, out_m).astype(BF), pad_m) + dot_nt(dot_nt(d_a, out_o).astype(BF), pad_o)
    d_qkv = vmem_call(
        attn_backward,
        jax.ShapeDtypeStruct((n, QKV), BF),
        [pltpu.VMEM((MB, ROT), F32)],
    )(d_o.astype(BF), rot, probs, cos, sin)

    def att_grad(h1_half, mixed_half):
        return jnp.concatenate([dot_tn(h1_half, d_qkv).astype(BF), dot_tn(mixed_half, d_a).astype(BF)], axis=1)

    g_att = reduce_gradient(att_grad(h1_m, mixed_m), att_grad(h1_o, mixed_o), PAD, "x")[:ROWS]
    dn1 = 0.0
    for w, p in ((qkv_m, pad_m), (qkv_o, pad_o)):
        for part in split(dot_nt(d_qkv, w)):
            dn1 = dn1 + dot_nt(part, p)
    grad_input = (d_x1 + s1 * dn1 - x * s1**3 * jnp.mean(dn1 * x, axis=-1, keepdims=True)).astype(BF)
    g_qkv = g_att[:, :QKV]
    g_norm_in = jnp.sum(g_qkv * s_qkv, axis=1)
    g_norm_mid = jnp.sum(g_gu * s_gu, axis=1)
    g_qkv = g_qkv * gain_in
    g_gu = g_gu * gain_mid
    return (
        layer_out,
        grad_input,
        g_norm_in,
        g_qkv[:, :D],
        g_qkv[:, D:ROT],
        g_qkv[:, ROT:],
        g_att[:, QKV:],
        g_norm_mid,
        g_gu[:, :FF],
        g_gu[:, FF:],
        g_down,
    )


def solution(mesh):
    rows = P(("dp", "outer"), None)
    ids = P(("dp", "outer"))
    vec = P("dp")
    mat = P("dp", None)
    in_specs = (rows, ids, vec, mat, mat, mat, mat, vec, mat, mat, mat, rows)
    out_specs = (rows, rows, vec, mat, mat, mat, mat, vec, mat, mat, mat)
    return jax.shard_map(local, mesh=mesh, in_specs=in_specs, out_specs=out_specs, check_vma=False)
```

```python
import math

import jax
import jax.numpy as jnp
from jax import lax
from jax.experimental import pallas as pl
from jax.experimental.pallas import tpu as pltpu
from jax.sharding import PartitionSpec as P

HEADS = 15
KV_HEADS = 5
SHARE = HEADS // KV_HEADS
HEAD_DIM = 64
MB = 128
DOCS = 4
D = 960
FF = 2560
QKV = 1600
ROT = 1280
NX = 4
NZ = 4
PIECES = 32
ROWS = 30
PAD = 32
DP = PIECES * PAD
HALF = DP // 2
DOWN = FF // PIECES

EPSILON = 1e-05
ROPE_BASE = 100000.0
BF = jnp.bfloat16
F32 = jnp.float32


def dot(a, b):
    return jnp.dot(a, b, preferred_element_type=F32)


def dot_nt(a, b):
    return lax.dot_general(a, b, (((1,), (1,)), ((), ())), preferred_element_type=F32)


def dot_tn(a, b):
    return lax.dot_general(a, b, (((0,), (0,)), ((), ())), preferred_element_type=F32)


def rms_scale(v):
    return lax.rsqrt(jnp.mean(v * v, axis=-1, keepdims=True) + EPSILON)


def swap_halves(v):
    n = v.shape[1]
    lane = lax.broadcasted_iota(jnp.int32, v.shape, 1)
    return jnp.where(lane % HEAD_DIM < HEAD_DIM // 2, pltpu.roll(v, n - 32, 1), pltpu.roll(v, 32, 1))


def forward(h1m_ref, h1o_ref, qm_ref, qo_ref, cos_ref, sin_ref, segc_ref, segr_ref, x_ref, om_ref, oo_ref,
            pm_ref, po_ref, nat_ref, rot_ref, prob_ref, mm_ref, mo_ref, x1_ref, h2_ref, qkv_ref, out_ref):
    qkv_ref[...] = dot(h1m_ref[...], qm_ref[...]) + dot(h1o_ref[...], qo_ref[...])
    blocks = qkv_ref.shape[0] // MB
    for b in range(blocks):
        rows = slice(b * MB, (b + 1) * MB)
        raw = qkv_ref[rows, :ROT]
        cos = jnp.concatenate([cos_ref[rows, :]] * (ROT // 128), axis=1)
        sin = jnp.concatenate([sin_ref[rows, :]] * (ROT // 128), axis=1)
        rot_ref[rows, :ROT] = (raw * cos + swap_halves(raw) * sin).astype(BF)
        rot_ref[rows, ROT:] = qkv_ref[rows, ROT:].astype(BF)
        r = lax.broadcasted_iota(jnp.int32, (MB, MB), 0)
        t = lax.broadcasted_iota(jnp.int32, (MB, MB), 1)
        allowed = (segc_ref[rows, :] == segr_ref[b : b + 1, :]) & (r >= t)
        allowed = jnp.concatenate([allowed] * SHARE, axis=0)
        for g in range(KV_HEADS):
            q = jnp.concatenate(
                [rot_ref[rows, (g * SHARE + j) * HEAD_DIM : (g * SHARE + j + 1) * HEAD_DIM] for j in range(SHARE)],
                axis=0,
            )
            k = rot_ref[rows, D + g * HEAD_DIM : D + (g + 1) * HEAD_DIM]
            v = rot_ref[rows, ROT + g * HEAD_DIM : ROT + (g + 1) * HEAD_DIM]
            s = jnp.where(allowed, dot_nt(q, k) * HEAD_DIM ** (-0.5), -1e30)
            e = jnp.exp(s - jnp.max(s, axis=-1, keepdims=True))
            p = e / jnp.sum(e, axis=-1, keepdims=True)
            at = (b * KV_HEADS + g) * SHARE * MB
            prob_ref[at : at + SHARE * MB, :] = p
            o = dot(p.astype(BF), v).astype(BF)
            for j in range(SHARE):
                h = g * SHARE + j
                out_ref[rows, h * HEAD_DIM : (h + 1) * HEAD_DIM] = o[j * MB : (j + 1) * MB, :]
    mm_ref[...] = dot(out_ref[...], pm_ref[...]).astype(BF)
    mo_ref[...] = dot(out_ref[...], po_ref[...]).astype(BF)
    x1 = x_ref[...].astype(F32) + dot(mm_ref[...], om_ref[...]) + dot(mo_ref[...], oo_ref[...])
    x1_ref[...] = x1
    h2_ref[...] = dot((x1 * rms_scale(x1)).astype(BF), nat_ref[...]).astype(BF)


def split(v):
    high = v.astype(BF)
    return high, (v - high.astype(F32)).astype(BF)


def backward_out(dh_ref, x1_ref, e_ref, nat_ref, om_ref, oo_ref, mm_ref, mo_ref, pm_ref, po_ref,
                 go_ref, gm_ref, dx1_ref, do_ref):
    high, low = split(dh_ref[...])
    dn = dot_nt(high, nat_ref[...]) + dot_nt(low, nat_ref[...])
    x1 = x1_ref[...]
    s2 = rms_scale(x1)
    dx1 = e_ref[...].astype(F32) + s2 * dn - x1 * (s2 * s2 * s2) * jnp.mean(dn * x1, axis=-1, keepdims=True)
    dx1_ref[...] = dx1
    da = dx1.astype(BF)
    go_ref[...] = dot_tn(mo_ref[...], da).astype(BF)
    gm_ref[...] = dot_tn(mm_ref[...], da).astype(BF)
    dm = dot_nt(da, om_ref[...]).astype(BF)
    dt = dot_nt(da, oo_ref[...]).astype(BF)
    do_ref[...] = (dot_nt(dm, pm_ref[...]) + dot_nt(dt, po_ref[...])).astype(BF)


def backward_attn(do_ref, rot_ref, prob_ref, cos_ref, sin_ref, h1m_ref, h1o_ref, wait_ref,
                  dqkv_ref, gm_ref, go_ref, work_ref):
    del wait_ref
    blocks = do_ref.shape[0] // MB
    scale = HEAD_DIM ** (-0.5)
    for b in range(blocks):
        rows = slice(b * MB, (b + 1) * MB)
        for g in range(KV_HEADS):
            heads = [slice((g * SHARE + j) * HEAD_DIM, (g * SHARE + j + 1) * HEAD_DIM) for j in range(SHARE)]
            q = jnp.concatenate([rot_ref[rows, h] for h in heads], axis=0)
            do = jnp.concatenate([do_ref[rows, h] for h in heads], axis=0)
            k = rot_ref[rows, D + g * HEAD_DIM : D + (g + 1) * HEAD_DIM]
            v = rot_ref[rows, ROT + g * HEAD_DIM : ROT + (g + 1) * HEAD_DIM]
            at = (b * KV_HEADS + g) * SHARE * MB
            p = prob_ref[at : at + SHARE * MB, :]
            dp = dot_nt(do, v)
            dv = dot_tn(p.astype(BF), do)
            delta = jnp.sum(p * dp, axis=-1, keepdims=True)
            ds = (p * (dp - delta)).astype(BF)
            dq = dot(ds, k) * scale
            dk = dot_tn(ds, q) * scale
            for j in range(SHARE):
                work_ref[:, heads[j]] = dq[j * MB : (j + 1) * MB, :]
            work_ref[:, D + g * HEAD_DIM : D + (g + 1) * HEAD_DIM] = dk
            dqkv_ref[rows, ROT + g * HEAD_DIM : ROT + (g + 1) * HEAD_DIM] = dv.astype(BF)
        cos = jnp.concatenate([cos_ref[rows, :]] * (ROT // 128), axis=1)
        sin = jnp.concatenate([sin_ref[rows, :]] * (ROT // 128), axis=1)
        w = work_ref[...]
        dqkv_ref[rows, :ROT] = (w * cos - swap_halves(w) * sin).astype(BF)
    go_ref[...] = dot_tn(h1o_ref[...], dqkv_ref[...]).astype(BF)
    gm_ref[...] = dot_tn(h1m_ref[...], dqkv_ref[...]).astype(BF)


def rope_tables(segment):
    n = segment.shape[0]
    seg = segment.reshape(n // MB, MB)
    index = lax.broadcasted_iota(jnp.int32, (n // MB, MB, MB), 2)
    same = seg[:, :, None] == seg[:, None, :]
    first = jnp.min(jnp.where(same, index, MB), axis=2)
    place = (jnp.arange(MB, dtype=jnp.int32)[None, :] - first).astype(F32).reshape(n, 1)
    lane = jnp.arange(128, dtype=jnp.int32)
    freq = jnp.exp((lane % 32).astype(F32) * (-2.0 * math.log(ROPE_BASE) / HEAD_DIM))
    angles = place * freq[None, :]
    sign = jnp.where(lane % 64 < 32, -1.0, 1.0)[None, :]
    return jnp.cos(angles), jnp.sin(angles) * sign


def padding_matrix(x, z, c):
    i = lax.broadcasted_iota(jnp.int32, (D, HALF), 0)
    j = lax.broadcasted_iota(jnp.int32, (D, HALF), 1)
    j_x = (x + j // (NZ * PAD)) % NX
    j_z = (z + j // PAD % NZ) % NZ
    j_r = j % PAD
    row = ((j_x * NZ + j_z) * 2 + c) * ROWS + j_r
    return ((i == row) & (j_r < ROWS)).astype(BF)


def natural_matrix():
    i = lax.broadcasted_iota(jnp.int32, (D, DP), 0)
    j = lax.broadcasted_iota(jnp.int32, (D, DP), 1)
    return ((i // ROWS) * PAD + i % ROWS == j).astype(BF)


def vmem_call(kernel, out_shape, flops, scratch=(), waits=0, count=0):
    extra = {}
    if waits:
        inside = [pl.BlockSpec(memory_space=pltpu.VMEM)] * count
        extra["in_specs"] = inside + [pl.BlockSpec(memory_space=pl.ANY)] * waits
    return pl.pallas_call(
        kernel,
        out_shape=out_shape,
        scratch_shapes=list(scratch),
        compiler_params=pltpu.CompilerParams(vmem_limit_bytes=48 * 1024 * 1024),
        cost_estimate=pl.CostEstimate(flops=flops, bytes_accessed=16 * 1024 * 1024, transcendentals=0),
        **extra,
    )


def place_of(x, z, c):
    return (x * NZ + z) * 2 + c


def shift(v, axis, s):
    perm = []
    for x in range(NX):
        for z in range(NZ):
            for c in range(2):
                to = {
                    "x": ((x + s) % NX, z, c),
                    "z": (x, (z + s) % NZ, c),
                    "c": (x, z, 1 - c),
                }[axis]
                perm.append((place_of(x, z, c), place_of(*to)))
    return lax.ppermute(v, "dp", perm)


def ring_gather(s, axis, cut=None):
    a = shift(s, axis, 1)
    b = shift(s, axis, -1)
    if cut is None:
        far = shift(s, axis, 2)
    else:
        far = jnp.concatenate([shift(a[:cut], axis, 1), shift(b[cut:], axis, -1)], axis=0)
    return [s, b, far, a]


def gather_half(s, first):
    second = "z" if first == "x" else "x"
    one = jnp.stack(ring_gather(s, first), axis=0)
    mine = jnp.stack(ring_gather(one, second, 2), axis=1 if first == "x" else 0)
    return mine, shift(mine, "c", 1)


def add_all(parts):
    total = parts[0].astype(F32)
    for p in parts[1:]:
        total = total + p.astype(F32)
    return total


def ring_sum(terms, axis):
    parts = [terms[0], shift(terms[2], axis, 2), shift(terms[1], axis, 1), shift(terms[3], axis, -1)]
    return add_all(parts).astype(BF)


def reduce_first(mine, other, rows, first):
    n = mine.shape[-1]
    got = shift(other, "c", 1).reshape(NX, NZ, rows, n)
    mine = mine.reshape(NX, NZ, rows, n)
    at = (lambda v, k: v[k]) if first == "x" else (lambda v, k: v[:, k])
    return ring_sum([add_all([at(mine, k), at(got, k)]).astype(BF) for k in range(4)], first)


def reduce_last(h, second):
    if second is not None:
        h = ring_sum([h[k] for k in range(4)], second)
    h = h + lax.ppermute(h, "outer", [(0, 1), (1, 0), (2, 3), (3, 2)])
    return add_all([h, lax.ppermute(h, "outer", [(0, 3), (3, 0), (1, 2), (2, 1)])])


def mlp(pos, h2_ref, e_ref, x1_ref, live_ref, gu_ref, down_ref,
        out_ref, gg_ref, gm_ref, go_ref, dh_ref, acc_ref, w_ref, g_ref, ht_ref):
    step = pl.program_id(0)
    z, c = pos[1], pos[2]
    tile = FF // NX

    @pl.when(step == 0)
    def _():
        ht_ref[...] = h2_ref[...].T

    for p in range(2 * NZ):
        for b in range(DOWN // 16):
            w_ref[p * DOWN + 16 * b : p * DOWN + 16 * b + 16, :] = down_ref[p, :, 1024 * b : 1024 * b + D]
    h2 = h2_ref[...]
    e = e_ref[...]
    wgu = gu_ref[...].reshape(DP, 2 * tile)
    both = dot(h2, wgu)
    gate, up = both[:, :tile], both[:, tile:]
    sig = jax.nn.sigmoid(gate)
    silu = gate * sig
    hidden = (silu * up).astype(BF)
    g_ref[...] = dot_tn(hidden, e)
    for kz in range(NZ):
        at = lax.rem(z + kz, NZ) * (2 * DOWN)
        gm_ref[0, kz] = g_ref[pl.ds(pl.multiple_of(at + c * DOWN, 16), DOWN), :].astype(BF)
        go_ref[0, kz] = g_ref[pl.ds(pl.multiple_of(at + (1 - c) * DOWN, 16), DOWN), :].astype(BF)
    d_hidden = dot_nt(e, w_ref[...])
    d_gate = (d_hidden * up * sig * (1.0 + gate * (1.0 - sig))).astype(BF)
    d_up = (d_hidden * silu).astype(BF)
    d_gu = jnp.concatenate([d_gate, d_up], axis=1)
    gg_ref[...] = dot(ht_ref[...], d_gu).astype(BF)
    dh = dot_nt(d_gu, wgu)
    y = dot(hidden, w_ref[...])

    @pl.when(step == 0)
    def _():
        dh_ref[...] = dh
        acc_ref[...] = x1_ref[...] + y

    @pl.when(step > 0)
    def _():
        dh_ref[...] += dh
        acc_ref[...] += y

    @pl.when(step == NX - 1)
    def _():
        out_ref[...] = (acc_ref[...] * live_ref[...]).astype(BF)


def mlp_call(pos, h2, e, x1, live, packed):
    n = h2.shape[0]
    tile = FF // NX

    def whole(a):
        return pl.BlockSpec(a.shape, lambda k, pos: (0,) * a.ndim)

    def here(k, pos):
        return lax.rem(pos[0] + k, NX)

    part = pl.BlockSpec((1, NZ, DOWN, D), lambda k, pos: (k, 0, 0, 0))
    return pl.pallas_call(
        mlp,
        out_shape=(
            jax.ShapeDtypeStruct((n, D), BF),
            jax.ShapeDtypeStruct((DP, 2 * FF), BF),
            jax.ShapeDtypeStruct((NX, NZ, DOWN, D), BF),
            jax.ShapeDtypeStruct((NX, NZ, DOWN, D), BF),
            jax.ShapeDtypeStruct((n, DP), F32),
        ),
        grid_spec=pltpu.PrefetchScalarGridSpec(
            num_scalar_prefetch=1,
            grid=(NX,),
            in_specs=[
                whole(h2),
                whole(e),
                whole(x1),
                whole(live),
                pl.BlockSpec((PIECES, PAD, 2 * tile), lambda k, pos: (0, 0, here(k, pos))),
                pl.BlockSpec((2 * NZ, 16, 2 * FF), lambda k, pos: (here(k, pos), 2, 0)),
            ],
            out_specs=(
                pl.BlockSpec((n, D), lambda k, pos: (0, 0)),
                pl.BlockSpec((DP, 2 * tile), lambda k, pos: (0, here(k, pos))),
                part,
                part,
                pl.BlockSpec((n, DP), lambda k, pos: (0, 0)),
            ),
            scratch_shapes=[
                pltpu.VMEM((n, D), F32),
                pltpu.VMEM((tile, D), BF),
                pltpu.VMEM((tile, D), F32),
                pltpu.VMEM((DP, n), BF),
            ],
        ),
        compiler_params=pltpu.CompilerParams(
            vmem_limit_bytes=56 * 1024 * 1024, dimension_semantics=("arbitrary",)
        ),
        cost_estimate=pl.CostEstimate(flops=18 * n * D * FF, bytes_accessed=40 * 1024 * 1024, transcendentals=n * FF),
    )(pos, h2, e, x1, live, packed, packed)


def pad_rows(w):
    return jnp.pad(w, ((0, PAD - ROWS), (0, 0)))


def weave(a, b):
    tile = FF // NX
    return jnp.concatenate([v[:, k * tile : (k + 1) * tile] for k in range(NX) for v in (a, b)], axis=1)


def unweave(v, which):
    tile = FF // NX
    return jnp.concatenate([v[:, (2 * k + which) * tile : (2 * k + which + 1) * tile] for k in range(NX)], axis=1)


def local(
    tokens_in,
    segment_ids,
    norm_in,
    w_query,
    w_key,
    w_value,
    w_out,
    norm_mid,
    w_gate,
    w_up,
    w_down,
    out_cotangent,
):
    n = tokens_in.shape[0]
    me = lax.axis_index("dp")
    c_at = me % 2
    z_at = (me // 2) % NZ
    x_at = me // (2 * NZ)
    pos = jnp.stack([x_at, z_at, c_at]).astype(jnp.int32)
    gain_in = norm_in.astype(F32)[:, None]
    gain_mid = norm_mid.astype(F32)[:, None]
    s_qkv = jnp.concatenate([w_query, w_key, w_value], axis=1).astype(F32)
    s_gu = weave(w_gate, w_up).astype(F32)
    down = jnp.pad(w_down, ((0, 0), (0, 1024 - D)))
    down = jnp.concatenate([down[16 * b : 16 * b + 16] for b in range(DOWN // 16)], axis=1)
    packed = jnp.concatenate([pad_rows((s_gu * gain_mid).astype(BF)), down], axis=0)
    packed = lax.all_gather(packed, "dp", axis=0, tiled=False)
    qkv_m, qkv_o = gather_half(pad_rows((s_qkv * gain_in).astype(BF)), "x")
    out_m, out_o = gather_half(pad_rows(w_out), "z")
    qkv_m, qkv_o = qkv_m.reshape(HALF, QKV), qkv_o.reshape(HALF, QKV)
    out_m, out_o = out_m.reshape(HALF, D), out_o.reshape(HALF, D)

    pad_m = padding_matrix(x_at, z_at, c_at)
    pad_o = padding_matrix(x_at, z_at, 1 - c_at)
    natural = natural_matrix()
    cos, sin = rope_tables(segment_ids)
    live = (segment_ids < DOCS).astype(F32)[:, None]
    e_low = (out_cotangent.astype(F32) * live).astype(BF)
    x = tokens_in.astype(F32)
    s1 = rms_scale(x)
    h1 = (x * s1).astype(BF)
    h1_m, h1_o = dot(h1, pad_m).astype(BF), dot(h1, pad_o).astype(BF)
    rot, probs, mixed_m, mixed_o, x1, h2 = vmem_call(
        forward,
        (
            jax.ShapeDtypeStruct((n, QKV), BF),
            jax.ShapeDtypeStruct((n * HEADS, MB), F32),
            jax.ShapeDtypeStruct((n, HALF), BF),
            jax.ShapeDtypeStruct((n, HALF), BF),
            jax.ShapeDtypeStruct((n, D), F32),
            jax.ShapeDtypeStruct((n, DP), BF),
        ),
        20 * 10**9,
        [pltpu.VMEM((n, QKV), F32), pltpu.VMEM((n, D), BF)],
    )(h1_m, h1_o, qkv_m, qkv_o, cos, sin, segment_ids[:, None], segment_ids.reshape(n // MB, MB),
      tokens_in, out_m, out_o, pad_m, pad_o, natural)

    layer_out, g_gu, gd_m, gd_o, dh2 = mlp_call(pos, h2, e_low, x1, live, packed)
    g_gu = lax.psum_scatter(g_gu, "dp", scatter_dimension=0, tiled=True)
    g_down = reduce_first(gd_m, gd_o, DOWN, "x")
    g_out_o, g_out_m, d_x1, d_o = vmem_call(
        backward_out,
        (
            jax.ShapeDtypeStruct((HALF, D), BF),
            jax.ShapeDtypeStruct((HALF, D), BF),
            jax.ShapeDtypeStruct((n, D), F32),
            jax.ShapeDtypeStruct((n, D), BF),
        ),
        8 * 10**9,
    )(dh2, x1, e_low, natural, out_m, out_o, mixed_m, mixed_o, pad_m, pad_o)
    g_out = reduce_first(g_out_m, g_out_o, PAD, "z")
    d_qkv, g_qkv_m, g_qkv_o = vmem_call(
        backward_attn,
        (
            jax.ShapeDtypeStruct((n, QKV), BF),
            jax.ShapeDtypeStruct((HALF, QKV), BF),
            jax.ShapeDtypeStruct((HALF, QKV), BF),
        ),
        12 * 10**9,
        [pltpu.VMEM((MB, ROT), F32)],
        waits=1,
        count=7,
    )(d_o, rot, probs, cos, sin, h1_m, h1_o, g_down)
    g_qkv = reduce_first(g_qkv_m, g_qkv_o, PAD, "x")
    g_qkv = reduce_last(g_qkv, "z")[:ROWS]
    g_out = reduce_last(g_out, "x")[:ROWS]
    g_down = reduce_last(g_down, "z")
    g_gu = reduce_last(g_gu, None)[:ROWS]

    dn1 = 0.0
    for w, p in ((qkv_m, pad_m), (qkv_o, pad_o)):
        for part in split(dot_nt(d_qkv, w)):
            dn1 = dn1 + dot_nt(part, p)
    grad_input = (d_x1 + s1 * dn1 - x * s1**3 * jnp.mean(dn1 * x, axis=-1, keepdims=True)).astype(BF)
    g_norm_in = jnp.sum(g_qkv * s_qkv, axis=1)
    g_norm_mid = jnp.sum(g_gu * s_gu, axis=1)
    g_qkv = g_qkv * gain_in
    g_gu = g_gu * gain_mid
    return (
        layer_out,
        grad_input,
        g_norm_in,
        g_qkv[:, :D],
        g_qkv[:, D:ROT],
        g_qkv[:, ROT:],
        g_out,
        g_norm_mid,
        unweave(g_gu, 0),
        unweave(g_gu, 1),
        g_down,
    )


def solution(mesh):
    rows = P(("dp", "outer"), None)
    ids = P(("dp", "outer"))
    vec = P("dp")
    mat = P("dp", None)
    in_specs = (rows, ids, vec, mat, mat, mat, mat, vec, mat, mat, mat, rows)
    out_specs = (rows, rows, vec, mat, mat, mat, mat, vec, mat, mat, mat)
    return jax.shard_map(local, mesh=mesh, in_specs=in_specs, out_specs=out_specs, check_vma=False)
```

```python
import math

import jax
import jax.numpy as jnp
from jax import lax
from jax.experimental import pallas as pl
from jax.experimental.pallas import tpu as pltpu
from jax.sharding import PartitionSpec as P

HEADS = 15
KV_HEADS = 5
SHARE = HEADS // KV_HEADS
HEAD_DIM = 64
MB = 128
DOCS = 4
D = 960
FF = 2560
QKV = 1600
ROT = 1280
NX = 4
NZ = 4
PIECES = 32
ROWS = 30
PAD = 32
DP = PIECES * PAD
HALF = DP // 2
DOWN = FF // PIECES

EPSILON = 1e-05
ROPE_BASE = 100000.0
BF = jnp.bfloat16
F32 = jnp.float32


def dot(a, b):
    return jnp.dot(a, b, preferred_element_type=F32)


def dot_nt(a, b):
    return lax.dot_general(a, b, (((1,), (1,)), ((), ())), preferred_element_type=F32)


def dot_tn(a, b):
    return lax.dot_general(a, b, (((0,), (0,)), ((), ())), preferred_element_type=F32)


def rms_scale(v):
    return lax.rsqrt(jnp.mean(v * v, axis=-1, keepdims=True) + EPSILON)


def swap_halves(v):
    n = v.shape[1]
    lane = lax.broadcasted_iota(jnp.int32, v.shape, 1)
    return jnp.where(lane % HEAD_DIM < HEAD_DIM // 2, pltpu.roll(v, n - 32, 1), pltpu.roll(v, 32, 1))


def forward(h1m_ref, h1o_ref, qm_ref, qo_ref, cos_ref, sin_ref, segc_ref, segr_ref, x_ref, om_ref, oo_ref,
            pm_ref, po_ref, nat_ref, ring_ref, rot_ref, prob_ref, mm_ref, mo_ref, x1_ref, h2_ref, h2x_ref, h2z_ref,
            qkv_ref, out_ref):
    qkv_ref[...] = dot(h1m_ref[...], qm_ref[...]) + dot(h1o_ref[...], qo_ref[...])
    blocks = qkv_ref.shape[0] // MB
    for b in range(blocks):
        rows = slice(b * MB, (b + 1) * MB)
        raw = qkv_ref[rows, :ROT]
        cos = jnp.concatenate([cos_ref[rows, :]] * (ROT // 128), axis=1)
        sin = jnp.concatenate([sin_ref[rows, :]] * (ROT // 128), axis=1)
        rot_ref[rows, :ROT] = (raw * cos + swap_halves(raw) * sin).astype(BF)
        rot_ref[rows, ROT:] = qkv_ref[rows, ROT:].astype(BF)
        r = lax.broadcasted_iota(jnp.int32, (MB, MB), 0)
        t = lax.broadcasted_iota(jnp.int32, (MB, MB), 1)
        allowed = (segc_ref[rows, :] == segr_ref[b : b + 1, :]) & (r >= t)
        allowed = jnp.concatenate([allowed] * SHARE, axis=0)
        for g in range(KV_HEADS):
            q = jnp.concatenate(
                [rot_ref[rows, (g * SHARE + j) * HEAD_DIM : (g * SHARE + j + 1) * HEAD_DIM] for j in range(SHARE)],
                axis=0,
            )
            k = rot_ref[rows, D + g * HEAD_DIM : D + (g + 1) * HEAD_DIM]
            v = rot_ref[rows, ROT + g * HEAD_DIM : ROT + (g + 1) * HEAD_DIM]
            s = jnp.where(allowed, dot_nt(q, k) * HEAD_DIM ** (-0.5), -1e30)
            e = jnp.exp(s - jnp.max(s, axis=-1, keepdims=True))
            p = e / jnp.sum(e, axis=-1, keepdims=True)
            at = (b * KV_HEADS + g) * SHARE * MB
            prob_ref[at : at + SHARE * MB, :] = p
            o = dot(p.astype(BF), v).astype(BF)
            for j in range(SHARE):
                h = g * SHARE + j
                out_ref[rows, h * HEAD_DIM : (h + 1) * HEAD_DIM] = o[j * MB : (j + 1) * MB, :]
    mm_ref[...] = dot(out_ref[...], pm_ref[...]).astype(BF)
    mo_ref[...] = dot(out_ref[...], po_ref[...]).astype(BF)
    x1 = x_ref[...].astype(F32) + dot(mm_ref[...], om_ref[...]) + dot(mo_ref[...], oo_ref[...])
    x1_ref[...] = x1
    h2 = (x1 * rms_scale(x1)).astype(BF)
    h2_ref[...] = dot(h2, nat_ref[...]).astype(BF)
    h2x_ref[:, :HALF] = dot(h2, pm_ref[...]).astype(BF)
    h2x_ref[:, HALF:] = dot(h2, po_ref[...]).astype(BF)
    h2z_ref[...] = dot(h2, ring_ref[...]).astype(BF)


def split(v):
    high = v.astype(BF)
    return high, (v - high.astype(F32)).astype(BF)


def backward_out(dh_ref, x1_ref, e_ref, nat_ref, om_ref, oo_ref, pm_ref, po_ref, dx1_ref, da_ref, do_ref):
    high, low = split(dh_ref[...])
    dn = dot_nt(high, nat_ref[...]) + dot_nt(low, nat_ref[...])
    x1 = x1_ref[...]
    s2 = rms_scale(x1)
    dx1 = e_ref[...].astype(F32) + s2 * dn - x1 * (s2 * s2 * s2) * jnp.mean(dn * x1, axis=-1, keepdims=True)
    dx1_ref[...] = dx1
    da = dx1.astype(BF)
    da_ref[...] = da
    dm = dot_nt(da, om_ref[...]).astype(BF)
    dt = dot_nt(da, oo_ref[...]).astype(BF)
    do_ref[...] = (dot_nt(dm, pm_ref[...]) + dot_nt(dt, po_ref[...])).astype(BF)


def input_grad(dqkv_ref, qm_ref, qo_ref, pm_ref, po_ref, dx1_ref, x_ref, w1_ref, w2_ref, w3_ref, w4_ref, w5_ref, out_ref):
    del w1_ref, w2_ref, w3_ref, w4_ref, w5_ref
    dn = jnp.zeros(dx1_ref.shape, F32)
    for w_ref, p_ref in ((qm_ref, pm_ref), (qo_ref, po_ref)):
        for part in split(dot_nt(dqkv_ref[...], w_ref[...])):
            dn += dot_nt(part, p_ref[...])
    x = x_ref[...].astype(F32)
    s1 = rms_scale(x)
    mean = jnp.mean(dn * x, axis=-1, keepdims=True)
    out_ref[...] = (dx1_ref[...] + s1 * dn - x * (s1 * s1 * s1) * mean).astype(BF)


def attention_grads(h1m_ref, h1o_ref, dqkv_ref, da_ref, mm_ref, mo_ref, w1_ref, w2_ref, w3_ref, w4_ref, gm_ref, go_ref):
    del w1_ref, w2_ref, w3_ref, w4_ref
    for g_ref, h1_ref, m_ref in ((go_ref, h1o_ref, mo_ref), (gm_ref, h1m_ref, mm_ref)):
        g_ref[:, :QKV] = dot_tn(h1_ref[...], dqkv_ref[...]).astype(BF)
        g_ref[:, QKV:] = dot_tn(m_ref[...], da_ref[...]).astype(BF)


def backward_attn(do_ref, rot_ref, prob_ref, cos_ref, sin_ref, wait1_ref, wait2_ref, dqkv_ref, work_ref):
    del wait1_ref, wait2_ref
    blocks = do_ref.shape[0] // MB
    scale = HEAD_DIM ** (-0.5)
    for b in range(blocks):
        rows = slice(b * MB, (b + 1) * MB)
        for g in range(KV_HEADS):
            heads = [slice((g * SHARE + j) * HEAD_DIM, (g * SHARE + j + 1) * HEAD_DIM) for j in range(SHARE)]
            q = jnp.concatenate([rot_ref[rows, h] for h in heads], axis=0)
            do = jnp.concatenate([do_ref[rows, h] for h in heads], axis=0)
            k = rot_ref[rows, D + g * HEAD_DIM : D + (g + 1) * HEAD_DIM]
            v = rot_ref[rows, ROT + g * HEAD_DIM : ROT + (g + 1) * HEAD_DIM]
            at = (b * KV_HEADS + g) * SHARE * MB
            p = prob_ref[at : at + SHARE * MB, :]
            dp = dot_nt(do, v)
            dv = dot_tn(p.astype(BF), do)
            delta = jnp.sum(p * dp, axis=-1, keepdims=True)
            ds = (p * (dp - delta)).astype(BF)
            dq = dot(ds, k) * scale
            dk = dot_tn(ds, q) * scale
            for j in range(SHARE):
                work_ref[:, heads[j]] = dq[j * MB : (j + 1) * MB, :]
            work_ref[:, D + g * HEAD_DIM : D + (g + 1) * HEAD_DIM] = dk
            dqkv_ref[rows, ROT + g * HEAD_DIM : ROT + (g + 1) * HEAD_DIM] = dv.astype(BF)
        cos = jnp.concatenate([cos_ref[rows, :]] * (ROT // 128), axis=1)
        sin = jnp.concatenate([sin_ref[rows, :]] * (ROT // 128), axis=1)
        w = work_ref[...]
        dqkv_ref[rows, :ROT] = (w * cos - swap_halves(w) * sin).astype(BF)


def rope_tables(segment):
    n = segment.shape[0]
    seg = segment.reshape(n // MB, MB)
    index = lax.broadcasted_iota(jnp.int32, (n // MB, MB, MB), 2)
    same = seg[:, :, None] == seg[:, None, :]
    first = jnp.min(jnp.where(same, index, MB), axis=2)
    place = (jnp.arange(MB, dtype=jnp.int32)[None, :] - first).astype(F32).reshape(n, 1)
    lane = jnp.arange(128, dtype=jnp.int32)
    freq = jnp.exp((lane % 32).astype(F32) * (-2.0 * math.log(ROPE_BASE) / HEAD_DIM))
    angles = place * freq[None, :]
    sign = jnp.where(lane % 64 < 32, -1.0, 1.0)[None, :]
    return jnp.cos(angles), jnp.sin(angles) * sign


def padding_matrix(x, z, c, first="x"):
    i = lax.broadcasted_iota(jnp.int32, (D, HALF), 0)
    j = lax.broadcasted_iota(jnp.int32, (D, HALF), 1)
    slow, fast = j // (4 * PAD), j // PAD % 4
    j_x = (x + (slow if first == "x" else fast)) % NX
    j_z = (z + (fast if first == "x" else slow)) % NZ
    j_r = j % PAD
    row = ((j_x * NZ + j_z) * 2 + c) * ROWS + j_r
    return ((i == row) & (j_r < ROWS)).astype(BF)


def natural_matrix():
    i = lax.broadcasted_iota(jnp.int32, (D, DP), 0)
    j = lax.broadcasted_iota(jnp.int32, (D, DP), 1)
    return ((i // ROWS) * PAD + i % ROWS == j).astype(BF)


def vmem_call(kernel, out_shape, scratch=(), waits=0, count=0):
    extra = {}
    if waits:
        inside = [pl.BlockSpec(memory_space=pltpu.VMEM)] * count
        extra["in_specs"] = inside + [pl.BlockSpec(memory_space=pl.ANY)] * waits
    return pl.pallas_call(
        kernel,
        out_shape=out_shape,
        scratch_shapes=list(scratch),
        compiler_params=pltpu.CompilerParams(vmem_limit_bytes=48 * 1024 * 1024),
        cost_estimate=pl.CostEstimate(flops=1, bytes_accessed=1, transcendentals=0),
        **extra,
    )


def pass_on(v_ref, wait_ref, out_ref):
    del v_ref, wait_ref, out_ref


def after(v, wait):
    return pl.pallas_call(
        pass_on,
        out_shape=jax.ShapeDtypeStruct(v.shape, v.dtype),
        in_specs=[pl.BlockSpec(memory_space=pl.ANY)] * 2,
        out_specs=pl.BlockSpec(memory_space=pl.ANY),
        input_output_aliases={0: 0},
        cost_estimate=pl.CostEstimate(flops=1, bytes_accessed=1, transcendentals=0),
    )(v, wait)


def place_of(x, z, c):
    return (x * NZ + z) * 2 + c


def shift(v, axis, s):
    perm = []
    for x in range(NX):
        for z in range(NZ):
            for c in range(2):
                to = {
                    "x": ((x + s) % NX, z, c),
                    "z": (x, (z + s) % NZ, c),
                    "c": (x, z, 1 - c),
                }[axis]
                perm.append((place_of(x, z, c), place_of(*to)))
    return lax.ppermute(v, "dp", perm)


def ring_gather(s, axis, cut=None):
    a = shift(s, axis, 1)
    b = shift(s, axis, -1)
    if cut is None:
        far = shift(s, axis, 2)
    else:
        far = jnp.concatenate([shift(a[:cut], axis, 1), shift(b[cut:], axis, -1)], axis=0)
    return [s, b, far, a]


def gather_half(s, first):
    second = "z" if first == "x" else "x"
    one = jnp.stack(ring_gather(s, first), axis=0)
    mine = jnp.stack(ring_gather(one, second, 2), axis=1 if first == "x" else 0)
    return mine, shift(mine, "c", 1)


def add_all(parts):
    total = parts[0].astype(F32)
    for p in parts[1:]:
        total = total + p.astype(F32)
    return total


def ring_sum(terms, axis):
    parts = [terms[0], shift(terms[2], axis, 2), shift(terms[1], axis, 1), shift(terms[3], axis, -1)]
    return add_all(parts).astype(BF)


class Ring:
    def __init__(self, pairs, first):
        self.first = first
        self.parts = []
        for mine, other in pairs:
            n = mine.shape[-1]
            rows = mine.size // (16 * n)
            got = shift(other, "c", 1).reshape(4, 4, rows, n)
            self.parts.append((mine.reshape(4, 4, rows, n), got))

    def hold(self, wait):
        self.parts = [(mine, after(got, wait)) for mine, got in self.parts]

    def term(self, k):
        sums = [(mine[k].astype(F32) + got[k].astype(F32)).astype(BF) for mine, got in self.parts]
        return sums[0] if len(sums) == 1 else jnp.concatenate(sums, axis=1)

    def begin(self):
        self.two = self.term(2)
        self.a = shift(self.two[:2], self.first, 1)
        self.b = shift(self.two[2:], self.first, -1)

    def middle(self):
        one, three = self.term(1), self.term(3)
        self.one = jnp.concatenate([one[:2] + self.a, one[2:]], axis=0)
        self.three = jnp.concatenate([three[:2], three[2:] + self.b], axis=0)
        self.c = shift(self.one, self.first, 1)
        self.d = shift(self.three, self.first, -1)

    def finish(self, wait=None):
        c = self.c if wait is None else after(self.c, wait)
        self.half = add_all([self.term(0), c, self.d]).astype(BF)

    def second(self):
        self.piece = ring_sum([self.half[k] for k in range(4)], "z" if self.first == "x" else "x")


def sum_outer(h):
    h = h + lax.ppermute(h, "outer", [(0, 1), (1, 0), (2, 3), (3, 2)])
    return add_all([h, lax.ppermute(h, "outer", [(0, 3), (3, 0), (1, 2), (2, 1)])])


def mlp(pos, h2_ref, h2x_ref, h2z_ref, e_ref, x1_ref, live_ref, gu_ref, down_ref,
        out_ref, gxm_ref, gxo_ref, gzm_ref, gzo_ref, dxm_ref, dxo_ref, dzm_ref, dzo_ref, dh_ref,
        acc_ref, w_ref, g_ref, hx_ref, hz_ref):
    step = pl.program_id(0)
    z, c = pos[1], pos[2]
    tile = FF // NX

    @pl.when(step == 0)
    def _():
        hx_ref[...] = h2x_ref[...].T
        hz_ref[...] = h2z_ref[...].T

    for p in range(2 * NZ):
        for b in range(DOWN // 16):
            w_ref[p * DOWN + 16 * b : p * DOWN + 16 * b + 16, :] = down_ref[p, :, 1024 * b : 1024 * b + D]
    h2 = h2_ref[...]
    e = e_ref[...]
    wgu = gu_ref[...].reshape(DP, 2 * tile)
    both = dot(h2, wgu)
    gate, up = both[:, :tile], both[:, tile:]
    sig = jax.nn.sigmoid(gate)
    silu = gate * sig
    hidden = (silu * up).astype(BF)
    d_hidden = dot_nt(e, w_ref[...])
    d_gate = (d_hidden * up * sig * (1.0 + gate * (1.0 - sig))).astype(BF)
    d_up = (d_hidden * silu).astype(BF)
    g_ref[...] = dot_tn(hidden, e)
    blank = jnp.zeros((16, 1024 - D), BF)
    for kz in range(NZ):
        at = lax.rem(z + kz, NZ) * (2 * DOWN)
        for core, dx, dz in ((c, dxm_ref.at[0, kz], dzm_ref.at[kz, 0]), (1 - c, dxo_ref.at[0, kz], dzo_ref.at[kz, 0])):
            rows = [
                g_ref[pl.ds(pl.multiple_of(at + core * DOWN + 16 * b, 16), 16), :].astype(BF)
                for b in range(DOWN // 16)
            ]
            dx[:, :D] = rows[0]
            dx[:, D:1024] = blank
            dx[:, 1024 : 1024 + D] = rows[1]
            dx[:, 1024 + D : 2048] = blank
            dx[:, 2048:] = rows[2][:, :512]
            dz[:, : D - 512] = rows[2][:, 512:]
            dz[:, D - 512 : 512] = blank
            dz[:, 512 : 512 + D] = rows[3]
            dz[:, 512 + D : 1536] = blank
            dz[:, 1536 : 1536 + D] = rows[4]
            dz[:, 1536 + D :] = blank
    gxm_ref[...] = dot(hx_ref[:HALF, :], d_gate).astype(BF)
    gxo_ref[...] = dot(hx_ref[HALF:, :], d_gate).astype(BF)
    gzm_ref[...] = dot(hz_ref[:HALF, :], d_up).astype(BF)
    gzo_ref[...] = dot(hz_ref[HALF:, :], d_up).astype(BF)
    dh = dot_nt(jnp.concatenate([d_gate, d_up], axis=1), wgu)
    y = dot(hidden, w_ref[...])

    @pl.when(step == 0)
    def _():
        dh_ref[...] = dh
        acc_ref[...] = x1_ref[...] + y

    @pl.when(step > 0)
    def _():
        dh_ref[...] += dh
        acc_ref[...] += y

    @pl.when(step == NX - 1)
    def _():
        out_ref[...] = (acc_ref[...] * live_ref[...]).astype(BF)


def mlp_call(pos, h2, h2x, h2z, e, x1, live, packed):
    n = h2.shape[0]
    tile = FF // NX

    def whole(a):
        return pl.BlockSpec(a.shape, lambda k, pos: (0,) * a.ndim)

    def here(k, pos):
        return lax.rem(pos[0] + k, NX)

    cols = pl.BlockSpec((HALF, tile), lambda k, pos: (0, here(k, pos)))
    along_x = pl.BlockSpec((1, NZ, 16, FF), lambda k, pos: (k, 0, 0, 0))
    along_z = pl.BlockSpec((NZ, 1, 16, FF), lambda k, pos: (0, k, 0, 0))
    return pl.pallas_call(
        mlp,
        out_shape=(
            jax.ShapeDtypeStruct((n, D), BF),
            *[jax.ShapeDtypeStruct((HALF, FF), BF)] * 4,
            *[jax.ShapeDtypeStruct((4, 4, 16, FF), BF)] * 4,
            jax.ShapeDtypeStruct((n, DP), F32),
        ),
        grid_spec=pltpu.PrefetchScalarGridSpec(
            num_scalar_prefetch=1,
            grid=(NX,),
            in_specs=[
                whole(h2),
                whole(h2x),
                whole(h2z),
                whole(e),
                whole(x1),
                whole(live),
                pl.BlockSpec((PIECES, PAD, 2 * tile), lambda k, pos: (0, 0, here(k, pos))),
                pl.BlockSpec((2 * NZ, 16, 2 * FF), lambda k, pos: (here(k, pos), 2, 0)),
            ],
            out_specs=(
                pl.BlockSpec((n, D), lambda k, pos: (0, 0)),
                *[cols] * 4,
                *[along_x] * 2,
                *[along_z] * 2,
                pl.BlockSpec((n, DP), lambda k, pos: (0, 0)),
            ),
            scratch_shapes=[
                pltpu.VMEM((n, D), F32),
                pltpu.VMEM((tile, D), BF),
                pltpu.VMEM((tile, D), F32),
                pltpu.VMEM((DP, n), BF),
                pltpu.VMEM((DP, n), BF),
            ],
        ),
        compiler_params=pltpu.CompilerParams(
            vmem_limit_bytes=56 * 1024 * 1024, dimension_semantics=("arbitrary",)
        ),
        cost_estimate=pl.CostEstimate(flops=1, bytes_accessed=1, transcendentals=0),
    )(pos, h2, h2x, h2z, e, x1, live, packed, packed)


def pad_rows(w):
    return jnp.pad(w, ((0, PAD - ROWS), (0, 0)))


def weave(a, b):
    tile = FF // NX
    return jnp.concatenate([v[:, k * tile : (k + 1) * tile] for k in range(NX) for v in (a, b)], axis=1)


def local(
    tokens_in,
    segment_ids,
    norm_in,
    w_query,
    w_key,
    w_value,
    w_out,
    norm_mid,
    w_gate,
    w_up,
    w_down,
    out_cotangent,
):
    n = tokens_in.shape[0]
    me = lax.axis_index("dp")
    c_at = me % 2
    z_at = (me // 2) % NZ
    x_at = me // (2 * NZ)
    pos = jnp.stack([x_at, z_at, c_at]).astype(jnp.int32)
    gain_in = norm_in.astype(F32)[:, None]
    gain_mid = norm_mid.astype(F32)[:, None]
    s_qkv = jnp.concatenate([w_query, w_key, w_value], axis=1).astype(F32)
    s_gu = weave(w_gate, w_up).astype(F32)
    down = jnp.pad(w_down, ((0, 0), (0, 1024 - D)))
    down = jnp.concatenate([down[16 * b : 16 * b + 16] for b in range(DOWN // 16)], axis=1)
    packed = jnp.concatenate([pad_rows((s_gu * gain_mid).astype(BF)), down], axis=0)
    packed = lax.all_gather(packed, "dp", axis=0, tiled=False)
    qkv_m, qkv_o = gather_half(pad_rows((s_qkv * gain_in).astype(BF)), "x")
    out_m, out_o = gather_half(pad_rows(w_out), "z")
    qkv_m, qkv_o = qkv_m.reshape(HALF, QKV), qkv_o.reshape(HALF, QKV)
    out_m, out_o = out_m.reshape(HALF, D), out_o.reshape(HALF, D)

    pad_m = padding_matrix(x_at, z_at, c_at)
    pad_o = padding_matrix(x_at, z_at, 1 - c_at)
    natural = natural_matrix()
    ring = jnp.concatenate(
        [padding_matrix(x_at, z_at, c_at, "z"), padding_matrix(x_at, z_at, 1 - c_at, "z")], axis=1
    )
    cos, sin = rope_tables(segment_ids)
    live = (segment_ids < DOCS).astype(F32)[:, None]
    e_low = (out_cotangent.astype(F32) * live).astype(BF)
    x = tokens_in.astype(F32)
    s1 = rms_scale(x)
    h1 = (x * s1).astype(BF)
    h1_m, h1_o = dot(h1, pad_m).astype(BF), dot(h1, pad_o).astype(BF)
    rot, probs, mixed_m, mixed_o, x1, h2, h2x, h2z = vmem_call(
        forward,
        (
            jax.ShapeDtypeStruct((n, QKV), BF),
            jax.ShapeDtypeStruct((n * HEADS, MB), F32),
            jax.ShapeDtypeStruct((n, HALF), BF),
            jax.ShapeDtypeStruct((n, HALF), BF),
            jax.ShapeDtypeStruct((n, D), F32),
            jax.ShapeDtypeStruct((n, DP), BF),
            jax.ShapeDtypeStruct((n, DP), BF),
            jax.ShapeDtypeStruct((n, DP), BF),
        ),
        [pltpu.VMEM((n, QKV), F32), pltpu.VMEM((n, D), BF)],
    )(h1_m, h1_o, qkv_m, qkv_o, cos, sin, segment_ids[:, None], segment_ids.reshape(n // MB, MB),
      tokens_in, out_m, out_o, pad_m, pad_o, natural, ring)

    layer_out, gx_m, gx_o, gz_m, gz_o, dx_m, dx_o, dz_m, dz_o, dh2 = mlp_call(
        pos, h2, h2x, h2z, e_low, x1, live, packed
    )
    ring_x = Ring([(gx_m, gx_o), (dx_m, dx_o)], "x")
    ring_z = Ring([(gz_m, gz_o), (dz_m, dz_o)], "z")
    ring_x.begin()
    ring_z.begin()
    d_x1, d_a, d_o = vmem_call(
        backward_out,
        (
            jax.ShapeDtypeStruct((n, D), F32),
            jax.ShapeDtypeStruct((n, D), BF),
            jax.ShapeDtypeStruct((n, D), BF),
        ),
    )(dh2, x1, e_low, natural, out_m, out_o, pad_m, pad_o)
    d_qkv = vmem_call(
        backward_attn,
        jax.ShapeDtypeStruct((n, QKV), BF),
        [pltpu.VMEM((MB, ROT), F32)],
        waits=2,
        count=5,
    )(d_o, rot, probs, cos, sin, ring_x.two, ring_z.two)
    ga_m, ga_o = vmem_call(
        attention_grads,
        (jax.ShapeDtypeStruct((HALF, QKV + D), BF), jax.ShapeDtypeStruct((HALF, QKV + D), BF)),
        waits=4,
        count=6,
    )(h1_m, h1_o, d_qkv, d_a, mixed_m, mixed_o, ring_x.a, ring_x.b, ring_z.a, ring_z.b)
    ring_att = Ring([(ga_m, ga_o)], "x")
    ring_x.middle()
    ring_z.middle()
    grad_input = vmem_call(
        input_grad, jax.ShapeDtypeStruct((n, D), BF), waits=5, count=7
    )(d_qkv, qkv_m, qkv_o, pad_m, pad_o, d_x1, tokens_in, ring_x.one, ring_x.three, ring_z.one, ring_z.three, ga_o)
    ring_x.finish(grad_input)
    ring_z.finish(grad_input)
    ring_att.begin()
    ring_att.middle()
    ring_att.finish()
    ring_x.half = after(ring_x.half, ring_att.two)
    ring_z.half = after(ring_z.half, ring_att.two)
    ring_x.second()
    ring_z.second()
    ring_att.second()
    g_mlp = sum_outer(after(jnp.stack([ring_x.piece, ring_z.piece]), ring_att.one))
    g_att = sum_outer(ring_att.piece)[:ROWS]
    g_gate, g_up = g_mlp[0, :ROWS], g_mlp[1, :ROWS]
    gd_x, gd_z = g_mlp[0, PAD:], g_mlp[1, PAD:]
    g_down = jnp.concatenate(
        [
            gd_x[:, :D],
            gd_x[:, 1024 : 1024 + D],
            jnp.concatenate([gd_x[:, 2048:], gd_z[:, : D - 512]], axis=1),
            gd_z[:, 512 : 512 + D],
            gd_z[:, 1536 : 1536 + D],
        ],
        axis=0,
    )
    g_qkv, g_out = g_att[:, :QKV], g_att[:, QKV:]

    g_norm_in = jnp.sum(g_qkv * s_qkv, axis=1)
    g_norm_mid = jnp.sum(g_gate * w_gate.astype(F32) + g_up * w_up.astype(F32), axis=1)
    g_qkv = g_qkv * gain_in
    return (
        layer_out,
        grad_input,
        g_norm_in,
        g_qkv[:, :D],
        g_qkv[:, D:ROT],
        g_qkv[:, ROT:],
        g_out,
        g_norm_mid,
        g_gate * gain_mid,
        g_up * gain_mid,
        g_down,
    )


def solution(mesh):
    rows = P(("dp", "outer"), None)
    ids = P(("dp", "outer"))
    vec = P("dp")
    mat = P("dp", None)
    in_specs = (rows, ids, vec, mat, mat, mat, mat, vec, mat, mat, mat, rows)
    out_specs = (rows, rows, vec, mat, mat, mat, mat, vec, mat, mat, mat)
    return jax.shard_map(local, mesh=mesh, in_specs=in_specs, out_specs=out_specs, check_vma=False)
```

```python
import math

import jax
import jax.numpy as jnp
from jax import lax
from jax.experimental import pallas as pl
from jax.experimental.pallas import tpu as pltpu
from jax.sharding import PartitionSpec as P

HEADS = 15
KV_HEADS = 5
SHARE = HEADS // KV_HEADS
HEAD_DIM = 64
MB = 128
DOCS = 4
D = 960
FF = 2560
QKV = 1600
ROT = 1280
NX = 4
NZ = 4
PIECES = 32
ROWS = 30
PAD = 32
DP = PIECES * PAD
HALF = DP // 2
QUARTER = 640
DOWN = FF // PIECES

EPSILON = 1e-05
ROPE_BASE = 100000.0
BF = jnp.bfloat16
F32 = jnp.float32


def dot(a, b):
    return jnp.dot(a, b, preferred_element_type=F32)


def dot_nt(a, b):
    return lax.dot_general(a, b, (((1,), (1,)), ((), ())), preferred_element_type=F32)


def dot_tn(a, b):
    return lax.dot_general(a, b, (((0,), (0,)), ((), ())), preferred_element_type=F32)


def rms_scale(v):
    return lax.rsqrt(jnp.mean(v * v, axis=-1, keepdims=True) + EPSILON)


def swap_halves(v):
    n = v.shape[1]
    lane = lax.broadcasted_iota(jnp.int32, v.shape, 1)
    return jnp.where(lane % HEAD_DIM < HEAD_DIM // 2, pltpu.roll(v, n - 32, 1), pltpu.roll(v, 32, 1))


def forward(y_ref, h1m_ref, h1o_ref, am_ref, ao_ref, cos_ref, sin_ref, segc_ref, segr_ref, x_ref,
            pm_ref, po_ref, nat_ref, ring_ref, rot_ref, prob_ref, mm_ref, mo_ref, x1_ref, h2_ref, h2x_ref, h2z_ref,
            qm_ref, qo_ref, om_ref, oo_ref, qkv_ref, out_ref):
    at = [lax.rem(q + 4 - y_ref[0], 4) for q in range(4)]
    for a_ref, q_ref, o_ref in ((am_ref, qm_ref, om_ref), (ao_ref, qo_ref, oo_ref)):
        q_ref[:, :QUARTER] = a_ref[at[0]]
        q_ref[:, QUARTER:ROT] = a_ref[at[1]]
        two = a_ref[at[2]]
        q_ref[:, ROT:] = two[:, : QKV - ROT]
        o_ref[:, QUARTER:] = two[:, QKV - ROT :]
        o_ref[:, :QUARTER] = a_ref[at[3]]
    qkv_ref[...] = dot(h1m_ref[...], qm_ref[...]) + dot(h1o_ref[...], qo_ref[...])
    blocks = qkv_ref.shape[0] // MB
    for b in range(blocks):
        rows = slice(b * MB, (b + 1) * MB)
        raw = qkv_ref[rows, :ROT]
        cos = jnp.concatenate([cos_ref[rows, :]] * (ROT // 128), axis=1)
        sin = jnp.concatenate([sin_ref[rows, :]] * (ROT // 128), axis=1)
        rot_ref[rows, :ROT] = (raw * cos + swap_halves(raw) * sin).astype(BF)
        rot_ref[rows, ROT:] = qkv_ref[rows, ROT:].astype(BF)
        r = lax.broadcasted_iota(jnp.int32, (MB, MB), 0)
        t = lax.broadcasted_iota(jnp.int32, (MB, MB), 1)
        allowed = (segc_ref[rows, :] == segr_ref[b : b + 1, :]) & (r >= t)
        allowed = jnp.concatenate([allowed] * SHARE, axis=0)
        for g in range(KV_HEADS):
            q = jnp.concatenate(
                [rot_ref[rows, (g * SHARE + j) * HEAD_DIM : (g * SHARE + j + 1) * HEAD_DIM] for j in range(SHARE)],
                axis=0,
            )
            k = rot_ref[rows, D + g * HEAD_DIM : D + (g + 1) * HEAD_DIM]
            v = rot_ref[rows, ROT + g * HEAD_DIM : ROT + (g + 1) * HEAD_DIM]
            s = jnp.where(allowed, dot_nt(q, k) * HEAD_DIM ** (-0.5), -1e30)
            e = jnp.exp(s - jnp.max(s, axis=-1, keepdims=True))
            p = e / jnp.sum(e, axis=-1, keepdims=True)
            at = (b * KV_HEADS + g) * SHARE * MB
            prob_ref[at : at + SHARE * MB, :] = p
            o = dot(p.astype(BF), v).astype(BF)
            for j in range(SHARE):
                h = g * SHARE + j
                out_ref[rows, h * HEAD_DIM : (h + 1) * HEAD_DIM] = o[j * MB : (j + 1) * MB, :]
    mm_ref[...] = dot(out_ref[...], pm_ref[...]).astype(BF)
    mo_ref[...] = dot(out_ref[...], po_ref[...]).astype(BF)
    x1 = x_ref[...].astype(F32) + dot(mm_ref[...], om_ref[...]) + dot(mo_ref[...], oo_ref[...])
    x1_ref[...] = x1
    h2 = (x1 * rms_scale(x1)).astype(BF)
    h2_ref[...] = dot(h2, nat_ref[...]).astype(BF)
    h2x_ref[:, :HALF] = dot(h2, pm_ref[...]).astype(BF)
    h2x_ref[:, HALF:] = dot(h2, po_ref[...]).astype(BF)
    h2z_ref[...] = dot(h2, ring_ref[...]).astype(BF)


def split(v):
    high = v.astype(BF)
    return high, (v - high.astype(F32)).astype(BF)


def backward_out(dh_ref, x1_ref, e_ref, nat_ref, om_ref, oo_ref, pm_ref, po_ref, dx1_ref, da_ref, do_ref):
    high, low = split(dh_ref[...])
    dn = dot_nt(high, nat_ref[...]) + dot_nt(low, nat_ref[...])
    x1 = x1_ref[...]
    s2 = rms_scale(x1)
    dx1 = e_ref[...].astype(F32) + s2 * dn - x1 * (s2 * s2 * s2) * jnp.mean(dn * x1, axis=-1, keepdims=True)
    dx1_ref[...] = dx1
    da = dx1.astype(BF)
    da_ref[...] = da
    dm = dot_nt(da, om_ref[...]).astype(BF)
    dt = dot_nt(da, oo_ref[...]).astype(BF)
    do_ref[...] = (dot_nt(dm, pm_ref[...]) + dot_nt(dt, po_ref[...])).astype(BF)


def input_grad(dqkv_ref, qm_ref, qo_ref, pm_ref, po_ref, dx1_ref, x_ref, w1_ref, w2_ref, w3_ref, w4_ref, w5_ref, out_ref):
    del w1_ref, w2_ref, w3_ref, w4_ref, w5_ref
    dn = jnp.zeros(dx1_ref.shape, F32)
    for w_ref, p_ref in ((qm_ref, pm_ref), (qo_ref, po_ref)):
        for part in split(dot_nt(dqkv_ref[...], w_ref[...])):
            dn += dot_nt(part, p_ref[...])
    x = x_ref[...].astype(F32)
    s1 = rms_scale(x)
    mean = jnp.mean(dn * x, axis=-1, keepdims=True)
    out_ref[...] = (dx1_ref[...] + s1 * dn - x * (s1 * s1 * s1) * mean).astype(BF)


def attention_grads(h1m_ref, h1o_ref, dqkv_ref, da_ref, mm_ref, mo_ref, w1_ref, w2_ref, w3_ref, w4_ref, gm_ref, go_ref):
    del w1_ref, w2_ref, w3_ref, w4_ref
    for g_ref, h1_ref, m_ref in ((go_ref, h1o_ref, mo_ref), (gm_ref, h1m_ref, mm_ref)):
        g_ref[:, :QKV] = dot_tn(h1_ref[...], dqkv_ref[...]).astype(BF)
        g_ref[:, QKV:] = dot_tn(m_ref[...], da_ref[...]).astype(BF)


def backward_attn(do_ref, rot_ref, prob_ref, cos_ref, sin_ref, wait1_ref, wait2_ref, dqkv_ref, work_ref):
    del wait1_ref, wait2_ref
    blocks = do_ref.shape[0] // MB
    scale = HEAD_DIM ** (-0.5)
    for b in range(blocks):
        rows = slice(b * MB, (b + 1) * MB)
        for g in range(KV_HEADS):
            heads = [slice((g * SHARE + j) * HEAD_DIM, (g * SHARE + j + 1) * HEAD_DIM) for j in range(SHARE)]
            q = jnp.concatenate([rot_ref[rows, h] for h in heads], axis=0)
            do = jnp.concatenate([do_ref[rows, h] for h in heads], axis=0)
            k = rot_ref[rows, D + g * HEAD_DIM : D + (g + 1) * HEAD_DIM]
            v = rot_ref[rows, ROT + g * HEAD_DIM : ROT + (g + 1) * HEAD_DIM]
            at = (b * KV_HEADS + g) * SHARE * MB
            p = prob_ref[at : at + SHARE * MB, :]
            dp = dot_nt(do, v)
            dv = dot_tn(p.astype(BF), do)
            delta = jnp.sum(p * dp, axis=-1, keepdims=True)
            ds = (p * (dp - delta)).astype(BF)
            dq = dot(ds, k) * scale
            dk = dot_tn(ds, q) * scale
            for j in range(SHARE):
                work_ref[:, heads[j]] = dq[j * MB : (j + 1) * MB, :]
            work_ref[:, D + g * HEAD_DIM : D + (g + 1) * HEAD_DIM] = dk
            dqkv_ref[rows, ROT + g * HEAD_DIM : ROT + (g + 1) * HEAD_DIM] = dv.astype(BF)
        cos = jnp.concatenate([cos_ref[rows, :]] * (ROT // 128), axis=1)
        sin = jnp.concatenate([sin_ref[rows, :]] * (ROT // 128), axis=1)
        w = work_ref[...]
        dqkv_ref[rows, :ROT] = (w * cos - swap_halves(w) * sin).astype(BF)


def rope_tables(segment):
    n = segment.shape[0]
    seg = segment.reshape(n // MB, MB)
    index = lax.broadcasted_iota(jnp.int32, (n // MB, MB, MB), 2)
    same = seg[:, :, None] == seg[:, None, :]
    first = jnp.min(jnp.where(same, index, MB), axis=2)
    place = (jnp.arange(MB, dtype=jnp.int32)[None, :] - first).astype(F32).reshape(n, 1)
    lane = jnp.arange(128, dtype=jnp.int32)
    freq = jnp.exp((lane % 32).astype(F32) * (-2.0 * math.log(ROPE_BASE) / HEAD_DIM))
    angles = place * freq[None, :]
    sign = jnp.where(lane % 64 < 32, -1.0, 1.0)[None, :]
    return jnp.cos(angles), jnp.sin(angles) * sign


def padding_matrix(x, z, c, first="x"):
    i = lax.broadcasted_iota(jnp.int32, (D, HALF), 0)
    j = lax.broadcasted_iota(jnp.int32, (D, HALF), 1)
    slow, fast = j // (4 * PAD), j // PAD % 4
    j_x = (x + (slow if first == "x" else fast)) % NX
    j_z = (z + (fast if first == "x" else slow)) % NZ
    j_r = j % PAD
    row = ((j_x * NZ + j_z) * 2 + c) * ROWS + j_r
    return ((i == row) & (j_r < ROWS)).astype(BF)


def natural_matrix():
    i = lax.broadcasted_iota(jnp.int32, (D, DP), 0)
    j = lax.broadcasted_iota(jnp.int32, (D, DP), 1)
    return ((i // ROWS) * PAD + i % ROWS == j).astype(BF)


def vmem_call(kernel, out_shape, scratch=(), waits=0, count=0, smem=0):
    extra = {}
    if smem:
        extra["in_specs"] = [pl.BlockSpec(memory_space=pltpu.SMEM)] + [pl.BlockSpec(memory_space=pltpu.VMEM)] * 13
    if waits:
        inside = [pl.BlockSpec(memory_space=pltpu.VMEM)] * count
        extra["in_specs"] = inside + [pl.BlockSpec(memory_space=pl.ANY)] * waits
    return pl.pallas_call(
        kernel,
        out_shape=out_shape,
        scratch_shapes=list(scratch),
        compiler_params=pltpu.CompilerParams(vmem_limit_bytes=48 * 1024 * 1024),
        cost_estimate=pl.CostEstimate(flops=1, bytes_accessed=1, transcendentals=0),
        **extra,
    )


def pass_on(v_ref, *refs):
    del v_ref, refs


def after(v, *waits):
    return pl.pallas_call(
        pass_on,
        out_shape=jax.ShapeDtypeStruct(v.shape, v.dtype),
        in_specs=[pl.BlockSpec(memory_space=pl.ANY)] * (1 + len(waits)),
        out_specs=pl.BlockSpec(memory_space=pl.ANY),
        input_output_aliases={0: 0},
        cost_estimate=pl.CostEstimate(flops=1, bytes_accessed=1, transcendentals=0),
    )(v, *waits)


def add_terms(*refs):
    for j in range(2):
        gm_ref, gg_ref, dm_ref, dg_ref = refs[4 * j : 4 * j + 4]
        out_ref = refs[len(refs) - 2 + j]
        out_ref[0, :, :PAD, :] = (gm_ref[0].astype(F32) + gg_ref[0].astype(F32)).astype(BF)
        out_ref[0, :, PAD:, :] = (dm_ref[0].astype(F32) + dg_ref[0].astype(F32)).astype(BF)


def add_terms_call(ring_x, ring_z, first, count, *waits):
    arrays = [v for ring in (ring_x, ring_z) for part in ring.parts for v in part]
    return pl.pallas_call(
        add_terms,
        grid=(count,),
        out_shape=[jax.ShapeDtypeStruct((count, 4, PAD + 16, FF), BF)] * 2,
        in_specs=[pl.BlockSpec((1,) + v.shape[1:], lambda i: (first + 2 * i, 0, 0, 0)) for v in arrays]
        + [pl.BlockSpec(memory_space=pl.ANY)] * len(waits),
        out_specs=[pl.BlockSpec((1, 4, PAD + 16, FF), lambda i: (i, 0, 0, 0))] * 2,
        compiler_params=pltpu.CompilerParams(vmem_limit_bytes=48 * 1024 * 1024),
        cost_estimate=pl.CostEstimate(flops=1, bytes_accessed=1, transcendentals=0),
    )(*arrays, *waits)


def place_of(x, z, c):
    return (x * NZ + z) * 2 + c


def shift(v, axis, s):
    if axis == "y":
        return lax.ppermute(v, "outer", [(i, (i + s) % 4) for i in range(4)])
    perm = []
    for x in range(NX):
        for z in range(NZ):
            for c in range(2):
                to = {
                    "x": ((x + s) % NX, z, c),
                    "z": (x, (z + s) % NZ, c),
                    "c": (x, z, 1 - c),
                }[axis]
                perm.append((place_of(x, z, c), place_of(*to)))
    return lax.ppermute(v, "dp", perm)


def ring_gather(s, axis, cut=None, waits=()):
    a = shift(s, axis, 1)
    b = shift(s, axis, -1)
    if cut is None:
        far = shift(s, axis, 2)
    else:
        if waits:
            a = after(a, *waits)
        far = jnp.concatenate([shift(a[:cut], axis, 1), shift(b[cut:], axis, -1)], axis=0)
    return [s, b, far, a]


def gather_attention(quarters, y, waits):
    own = lax.dynamic_index_in_dim(quarters, y, 0, keepdims=False)
    one = jnp.stack(ring_gather(own, "x"), axis=0)
    two = jnp.stack(ring_gather(one, "z", 2), axis=1).reshape(HALF, QUARTER)
    mine = jnp.stack(ring_gather(two, "y", HALF // 2, waits), axis=0)
    return mine, shift(mine, "c", 1)


def add_all(parts):
    total = parts[0].astype(F32)
    for p in parts[1:]:
        total = total + p.astype(F32)
    return total


def ring_sum(terms, axis):
    parts = [terms[0], shift(terms[2], axis, 2), shift(terms[1], axis, 1), shift(terms[3], axis, -1)]
    return add_all(parts).astype(BF)


class Ring:
    def __init__(self, pairs, first):
        self.first = first
        self.parts = []
        for mine, other in pairs:
            n = mine.shape[-1]
            rows = mine.size // (16 * n)
            got = shift(other, "c", 1).reshape(4, 4, rows, n)
            self.parts.append((mine.reshape(4, 4, rows, n), got))

    def term(self, k):
        sums = [(mine[k].astype(F32) + got[k].astype(F32)).astype(BF) for mine, got in self.parts]
        return sums[0] if len(sums) == 1 else jnp.concatenate(sums, axis=1)

    def begin(self, two=None):
        self.two = self.term(2) if two is None else two
        self.a = shift(self.two[:2], self.first, 1)
        self.b = shift(self.two[2:], self.first, -1)

    def middle(self, one=None, three=None):
        one = self.term(1) if one is None else one
        three = self.term(3) if three is None else three
        self.one = jnp.concatenate([one[:2] + self.a, one[2:]], axis=0)
        self.three = jnp.concatenate([three[:2], three[2:] + self.b], axis=0)
        self.c = shift(self.one, self.first, 1)
        self.d = shift(self.three, self.first, -1)

    def finish(self, *waits):
        c = after(self.c, *waits) if waits else self.c
        self.half = add_all([self.term(0), c, self.d]).astype(BF)

    def second(self):
        self.piece = ring_sum([self.half[k] for k in range(4)], "z" if self.first == "x" else "x")


def sum_outer(h, turn):
    pairs = [[(0, 1), (1, 0), (2, 3), (3, 2)], [(0, 3), (3, 0), (1, 2), (2, 1)]]
    h = h + lax.ppermute(h, "outer", pairs[turn])
    return add_all([h, lax.ppermute(h, "outer", pairs[1 - turn])])


def mlp(pos, h2_ref, h2x_ref, h2z_ref, e_ref, x1_ref, live_ref, gu_ref, down_ref,
        out_ref, gxm_ref, gxo_ref, gzm_ref, gzo_ref, dxm_ref, dxo_ref, dzm_ref, dzo_ref, dh_ref,
        acc_ref, w_ref, g_ref, hx_ref, hz_ref):
    step = pl.program_id(0)
    z, c = pos[1], pos[2]
    tile = FF // NX

    @pl.when(step == 0)
    def _():
        hx_ref[...] = h2x_ref[...].T
        hz_ref[...] = h2z_ref[...].T

    for p in range(2 * NZ):
        for b in range(DOWN // 16):
            w_ref[p * DOWN + 16 * b : p * DOWN + 16 * b + 16, :] = down_ref[p, :, 1024 * b : 1024 * b + D]
    h2 = h2_ref[...]
    e = e_ref[...]
    wgu = gu_ref[...].reshape(DP, 2 * tile)
    both = dot(h2, wgu)
    gate, up = both[:, :tile], both[:, tile:]
    sig = jax.nn.sigmoid(gate)
    silu = gate * sig
    hidden = (silu * up).astype(BF)
    d_hidden = dot_nt(e, w_ref[...])
    d_gate = (d_hidden * up * sig * (1.0 + gate * (1.0 - sig))).astype(BF)
    d_up = (d_hidden * silu).astype(BF)
    g_ref[...] = dot_tn(hidden, e)
    blank = jnp.zeros((16, 1024 - D), BF)
    for kz in range(NZ):
        at = lax.rem(z + kz, NZ) * (2 * DOWN)
        for core, dx, dz in ((c, dxm_ref.at[0, kz], dzm_ref.at[kz, 0]), (1 - c, dxo_ref.at[0, kz], dzo_ref.at[kz, 0])):
            rows = [
                g_ref[pl.ds(pl.multiple_of(at + core * DOWN + 16 * b, 16), 16), :].astype(BF)
                for b in range(DOWN // 16)
            ]
            dx[:, :D] = rows[0]
            dx[:, D:1024] = blank
            dx[:, 1024 : 1024 + D] = rows[1]
            dx[:, 1024 + D : 2048] = blank
            dx[:, 2048:] = rows[2][:, :512]
            dz[:, : D - 512] = rows[2][:, 512:]
            dz[:, D - 512 : 512] = blank
            dz[:, 512 : 512 + D] = rows[3]
            dz[:, 512 + D : 1536] = blank
            dz[:, 1536 : 1536 + D] = rows[4]
            dz[:, 1536 + D :] = blank
    gxm_ref[...] = dot(hx_ref[:HALF, :], d_gate).astype(BF)
    gxo_ref[...] = dot(hx_ref[HALF:, :], d_gate).astype(BF)
    gzm_ref[...] = dot(hz_ref[:HALF, :], d_up).astype(BF)
    gzo_ref[...] = dot(hz_ref[HALF:, :], d_up).astype(BF)
    dh = dot_nt(jnp.concatenate([d_gate, d_up], axis=1), wgu)
    y = dot(hidden, w_ref[...])

    @pl.when(step == 0)
    def _():
        dh_ref[...] = dh
        acc_ref[...] = x1_ref[...] + y

    @pl.when(step > 0)
    def _():
        dh_ref[...] += dh
        acc_ref[...] += y

    @pl.when(step == NX - 1)
    def _():
        out_ref[...] = (acc_ref[...] * live_ref[...]).astype(BF)


def mlp_call(pos, h2, h2x, h2z, e, x1, live, packed):
    n = h2.shape[0]
    tile = FF // NX

    def whole(a):
        return pl.BlockSpec(a.shape, lambda k, pos: (0,) * a.ndim)

    def here(k, pos):
        return lax.rem(pos[0] + k, NX)

    cols = pl.BlockSpec((HALF, tile), lambda k, pos: (0, here(k, pos)))
    along_x = pl.BlockSpec((1, NZ, 16, FF), lambda k, pos: (k, 0, 0, 0))
    along_z = pl.BlockSpec((NZ, 1, 16, FF), lambda k, pos: (0, k, 0, 0))
    return pl.pallas_call(
        mlp,
        out_shape=(
            jax.ShapeDtypeStruct((n, D), BF),
            *[jax.ShapeDtypeStruct((HALF, FF), BF)] * 4,
            *[jax.ShapeDtypeStruct((4, 4, 16, FF), BF)] * 4,
            jax.ShapeDtypeStruct((n, DP), F32),
        ),
        grid_spec=pltpu.PrefetchScalarGridSpec(
            num_scalar_prefetch=1,
            grid=(NX,),
            in_specs=[
                whole(h2),
                whole(h2x),
                whole(h2z),
                whole(e),
                whole(x1),
                whole(live),
                pl.BlockSpec((PIECES, PAD, 2 * tile), lambda k, pos: (0, 0, here(k, pos))),
                pl.BlockSpec((2 * NZ, 16, 2 * FF), lambda k, pos: (here(k, pos), 2, 0)),
            ],
            out_specs=(
                pl.BlockSpec((n, D), lambda k, pos: (0, 0)),
                *[cols] * 4,
                *[along_x] * 2,
                *[along_z] * 2,
                pl.BlockSpec((n, DP), lambda k, pos: (0, 0)),
            ),
            scratch_shapes=[
                pltpu.VMEM((n, D), F32),
                pltpu.VMEM((tile, D), BF),
                pltpu.VMEM((tile, D), F32),
                pltpu.VMEM((DP, n), BF),
                pltpu.VMEM((DP, n), BF),
            ],
        ),
        compiler_params=pltpu.CompilerParams(
            vmem_limit_bytes=56 * 1024 * 1024, dimension_semantics=("arbitrary",)
        ),
        cost_estimate=pl.CostEstimate(flops=1, bytes_accessed=1, transcendentals=0),
    )(pos, h2, h2x, h2z, e, x1, live, packed, packed)


def pack(gi_ref, gm_ref, wq_ref, wk_ref, wv_ref, wo_ref, wg_ref, wu_ref, wd_ref, att_ref, packed_ref):
    tile = FF // NX

    def padded(v):
        return jnp.concatenate([v, jnp.zeros((PAD - ROWS, v.shape[1]), F32)], axis=0).astype(BF)

    gi, gm = gi_ref[...], gm_ref[...]
    qkv = jnp.concatenate([wq_ref[...], wk_ref[...], wv_ref[...]], axis=1).astype(F32)
    qkv = padded(qkv * gi)
    out = padded(wo_ref[...].astype(F32))
    att_ref[0] = qkv[:, :QUARTER]
    att_ref[1] = qkv[:, QUARTER:ROT]
    att_ref[2] = jnp.concatenate([qkv[:, ROT:], out[:, QUARTER:]], axis=1)
    att_ref[3] = out[:, :QUARTER]
    for k in range(NX):
        for j, w_ref in enumerate((wg_ref, wu_ref)):
            at = (2 * k + j) * tile
            packed_ref[:PAD, at : at + tile] = padded(w_ref[:, k * tile : (k + 1) * tile].astype(F32) * gm)
    for b in range(DOWN // 16):
        rows = wd_ref[16 * b : 16 * b + 16, :]
        packed_ref[PAD:, 1024 * b : 1024 * (b + 1)] = jnp.concatenate([rows, jnp.zeros((16, 1024 - D), BF)], axis=1)


def local(
    tokens_in,
    segment_ids,
    norm_in,
    w_query,
    w_key,
    w_value,
    w_out,
    norm_mid,
    w_gate,
    w_up,
    w_down,
    out_cotangent,
):
    n = tokens_in.shape[0]
    me = lax.axis_index("dp")
    c_at = me % 2
    z_at = (me // 2) % NZ
    x_at = me // (2 * NZ)
    pos = jnp.stack([x_at, z_at, c_at]).astype(jnp.int32)
    gain_in = norm_in.astype(F32)[:, None]
    gain_mid = norm_mid.astype(F32)[:, None]
    s_qkv = jnp.concatenate([w_query, w_key, w_value], axis=1).astype(F32)
    quarters, packed = vmem_call(
        pack,
        (
            jax.ShapeDtypeStruct((4, PAD, QUARTER), BF),
            jax.ShapeDtypeStruct((PAD + 16, 2 * FF), BF),
        ),
    )(gain_in, gain_mid, w_query, w_key, w_value, w_out, w_gate, w_up, w_down)
    packed = lax.all_gather(packed, "dp", axis=0, tiled=False)
    y_at = lax.axis_index("outer").astype(jnp.int32)
    pad_m = padding_matrix(x_at, z_at, c_at)
    pad_o = padding_matrix(x_at, z_at, 1 - c_at)
    natural = natural_matrix()
    ring = jnp.concatenate(
        [padding_matrix(x_at, z_at, c_at, "z"), padding_matrix(x_at, z_at, 1 - c_at, "z")], axis=1
    )
    cos, sin = rope_tables(segment_ids)
    live = (segment_ids < DOCS).astype(F32)[:, None]
    e_low = (out_cotangent.astype(F32) * live).astype(BF)
    x = tokens_in.astype(F32)
    s1 = rms_scale(x)
    h1 = (x * s1).astype(BF)
    h1_m, h1_o = dot(h1, pad_m).astype(BF), dot(h1, pad_o).astype(BF)
    att_m, att_o = gather_attention(quarters, y_at, (natural, ring, h1_m, h1_o, cos, sin, e_low))
    rot, probs, mixed_m, mixed_o, x1, h2, h2x, h2z, qkv_m, qkv_o, out_m, out_o = vmem_call(
        forward,
        (
            jax.ShapeDtypeStruct((n, QKV), BF),
            jax.ShapeDtypeStruct((n * HEADS, MB), F32),
            jax.ShapeDtypeStruct((n, HALF), BF),
            jax.ShapeDtypeStruct((n, HALF), BF),
            jax.ShapeDtypeStruct((n, D), F32),
            jax.ShapeDtypeStruct((n, DP), BF),
            jax.ShapeDtypeStruct((n, DP), BF),
            jax.ShapeDtypeStruct((n, DP), BF),
            jax.ShapeDtypeStruct((HALF, QKV), BF),
            jax.ShapeDtypeStruct((HALF, QKV), BF),
            jax.ShapeDtypeStruct((HALF, D), BF),
            jax.ShapeDtypeStruct((HALF, D), BF),
        ),
        [pltpu.VMEM((n, QKV), F32), pltpu.VMEM((n, D), BF)],
            smem=1,
    )(y_at[None], h1_m, h1_o, att_m, att_o, cos, sin, segment_ids[:, None], segment_ids.reshape(n // MB, MB),
      tokens_in, pad_m, pad_o, natural, ring)

    layer_out, gx_m, gx_o, gz_m, gz_o, dx_m, dx_o, dz_m, dz_o, dh2 = mlp_call(
        pos, h2, h2x, h2z, e_low, x1, live, packed
    )
    ring_x = Ring([(gx_m, gx_o), (dx_m, dx_o)], "x")
    ring_z = Ring([(gz_m, gz_o), (dz_m, dz_o)], "z")
    two_x, two_z = add_terms_call(ring_x, ring_z, 2, 1)
    ring_x.begin(two_x[0])
    ring_z.begin(two_z[0])
    d_x1, d_a, d_o = vmem_call(
        backward_out,
        (
            jax.ShapeDtypeStruct((n, D), F32),
            jax.ShapeDtypeStruct((n, D), BF),
            jax.ShapeDtypeStruct((n, D), BF),
        ),
    )(dh2, x1, e_low, natural, out_m, out_o, pad_m, pad_o)
    d_qkv = vmem_call(
        backward_attn,
        jax.ShapeDtypeStruct((n, QKV), BF),
        [pltpu.VMEM((MB, ROT), F32)],
        waits=2,
        count=5,
    )(d_o, rot, probs, cos, sin, ring_x.two, ring_z.two)
    ga_m, ga_o = vmem_call(
        attention_grads,
        (jax.ShapeDtypeStruct((HALF, QKV + D), BF), jax.ShapeDtypeStruct((HALF, QKV + D), BF)),
        waits=4,
        count=6,
    )(h1_m, h1_o, d_qkv, d_a, mixed_m, mixed_o, ring_x.a, ring_x.b, ring_z.a, ring_z.b)
    rest_x, rest_z = add_terms_call(ring_x, ring_z, 1, 2, d_qkv)
    ring_att = Ring([(ga_m, ga_o)], "x")
    ring_x.middle(rest_x[0], rest_x[1])
    ring_z.middle(rest_z[0], rest_z[1])
    ring_att.begin()
    grad_input = vmem_call(
        input_grad, jax.ShapeDtypeStruct((n, D), BF), waits=5, count=7
    )(d_qkv, qkv_m, qkv_o, pad_m, pad_o, d_x1, tokens_in, ring_x.one, ring_x.three, ring_z.one, ring_z.three, ring_att.two)
    ring_x.finish(grad_input, ring_att.a)
    ring_z.finish(grad_input, ring_att.b)
    layer_out = after(layer_out, grad_input)
    ring_att.middle()
    ring_att.finish()
    ring_x.second()
    ring_z.second()
    ring_att.second()
    gd_x = sum_outer(after(ring_x.piece, ring_att.one), 0)
    gd_z = sum_outer(after(ring_z.piece, ring_att.one), 1)
    g_att = sum_outer(ring_att.piece, 0)[:ROWS]
    g_gate, g_up = gd_x[:ROWS], gd_z[:ROWS]
    gd_x, gd_z = gd_x[PAD:], gd_z[PAD:]
    g_down = jnp.concatenate(
        [
            gd_x[:, :D],
            gd_x[:, 1024 : 1024 + D],
            jnp.concatenate([gd_x[:, 2048:], gd_z[:, : D - 512]], axis=1),
            gd_z[:, 512 : 512 + D],
            gd_z[:, 1536 : 1536 + D],
        ],
        axis=0,
    )
    g_qkv, g_out = g_att[:, :QKV], g_att[:, QKV:]

    g_norm_in = jnp.sum(g_qkv * s_qkv, axis=1)
    g_norm_mid = jnp.sum(g_gate * w_gate.astype(F32) + g_up * w_up.astype(F32), axis=1)
    g_qkv = g_qkv * gain_in
    return (
        layer_out,
        grad_input,
        g_norm_in,
        g_qkv[:, :D],
        g_qkv[:, D:ROT],
        g_qkv[:, ROT:],
        g_out,
        g_norm_mid,
        g_gate * gain_mid,
        g_up * gain_mid,
        g_down,
    )


def solution(mesh):
    rows = P(("dp", "outer"), None)
    ids = P(("dp", "outer"))
    vec = P("dp")
    mat = P("dp", None)
    in_specs = (rows, ids, vec, mat, mat, mat, mat, vec, mat, mat, mat, rows)
    out_specs = (rows, rows, vec, mat, mat, mat, mat, vec, mat, mat, mat)
    return jax.shard_map(local, mesh=mesh, in_specs=in_specs, out_specs=out_specs, check_vma=False)
```

```python
import math

import jax
import jax.numpy as jnp
from jax import lax
from jax.experimental import pallas as pl
from jax.experimental.pallas import tpu as pltpu
from jax.sharding import PartitionSpec as P

HEADS = 15
KV_HEADS = 5
SHARE = HEADS // KV_HEADS
HEAD_DIM = 64
MB = 128
DOCS = 4
D = 960
FF = 2560
QKV = 1600
ROT = 1280
NX = 4
NZ = 4
PIECES = 32
ROWS = 30
PAD = 32
DP = PIECES * PAD
HALF = DP // 2
QUARTER = 640
DOWN = FF // PIECES

EPSILON = 1e-05
ROPE_BASE = 100000.0
BF = jnp.bfloat16
F32 = jnp.float32


def dot(a, b):
    return jnp.dot(a, b, preferred_element_type=F32)


def dot_nt(a, b):
    return lax.dot_general(a, b, (((1,), (1,)), ((), ())), preferred_element_type=F32)


def dot_tn(a, b):
    return lax.dot_general(a, b, (((0,), (0,)), ((), ())), preferred_element_type=F32)


def rms_scale(v):
    return lax.rsqrt(jnp.mean(v * v, axis=-1, keepdims=True) + EPSILON)


def swap_halves(v):
    n = v.shape[1]
    lane = lax.broadcasted_iota(jnp.int32, v.shape, 1)
    return jnp.where(lane % HEAD_DIM < HEAD_DIM // 2, pltpu.roll(v, n - 32, 1), pltpu.roll(v, 32, 1))


def forward(y_ref, h1m_ref, h1o_ref, am_ref, ao_ref, cos_ref, sin_ref, segc_ref, segr_ref, x_ref,
            pm_ref, po_ref, nat_ref, ring_ref, rot_ref, prob_ref, mm_ref, mo_ref, x1_ref, h2_ref, h2x_ref, h2z_ref,
            qm_ref, qo_ref, om_ref, oo_ref, qkv_ref, out_ref):
    at = [lax.rem(q + 4 - y_ref[0], 4) for q in range(4)]
    for a_ref, q_ref, o_ref in ((am_ref, qm_ref, om_ref), (ao_ref, qo_ref, oo_ref)):
        q_ref[:, :QUARTER] = a_ref[at[0]]
        q_ref[:, QUARTER:ROT] = a_ref[at[1]]
        two = a_ref[at[2]]
        q_ref[:, ROT:] = two[:, : QKV - ROT]
        o_ref[:, QUARTER:] = two[:, QKV - ROT :]
        o_ref[:, :QUARTER] = a_ref[at[3]]
    qkv_ref[...] = dot(h1m_ref[...], qm_ref[...]) + dot(h1o_ref[...], qo_ref[...])
    blocks = qkv_ref.shape[0] // MB
    for b in range(blocks):
        rows = slice(b * MB, (b + 1) * MB)
        raw = qkv_ref[rows, :ROT]
        cos = jnp.concatenate([cos_ref[rows, :]] * (ROT // 128), axis=1)
        sin = jnp.concatenate([sin_ref[rows, :]] * (ROT // 128), axis=1)
        rot_ref[rows, :ROT] = (raw * cos + swap_halves(raw) * sin).astype(BF)
        rot_ref[rows, ROT:] = qkv_ref[rows, ROT:].astype(BF)
        r = lax.broadcasted_iota(jnp.int32, (MB, MB), 0)
        t = lax.broadcasted_iota(jnp.int32, (MB, MB), 1)
        allowed = (segc_ref[rows, :] == segr_ref[b : b + 1, :]) & (r >= t)
        allowed = jnp.concatenate([allowed] * SHARE, axis=0)
        for g in range(KV_HEADS):
            q = jnp.concatenate(
                [rot_ref[rows, (g * SHARE + j) * HEAD_DIM : (g * SHARE + j + 1) * HEAD_DIM] for j in range(SHARE)],
                axis=0,
            )
            k = rot_ref[rows, D + g * HEAD_DIM : D + (g + 1) * HEAD_DIM]
            v = rot_ref[rows, ROT + g * HEAD_DIM : ROT + (g + 1) * HEAD_DIM]
            s = jnp.where(allowed, dot_nt(q, k) * HEAD_DIM ** (-0.5), -1e30)
            e = jnp.exp(s - jnp.max(s, axis=-1, keepdims=True))
            p = e / jnp.sum(e, axis=-1, keepdims=True)
            at = (b * KV_HEADS + g) * SHARE * MB
            prob_ref[at : at + SHARE * MB, :] = p
            o = dot(p.astype(BF), v).astype(BF)
            for j in range(SHARE):
                h = g * SHARE + j
                out_ref[rows, h * HEAD_DIM : (h + 1) * HEAD_DIM] = o[j * MB : (j + 1) * MB, :]
    mm_ref[...] = dot(out_ref[...], pm_ref[...]).astype(BF)
    mo_ref[...] = dot(out_ref[...], po_ref[...]).astype(BF)
    x1 = x_ref[...].astype(F32) + dot(mm_ref[...], om_ref[...]) + dot(mo_ref[...], oo_ref[...])
    x1_ref[...] = x1
    h2 = (x1 * rms_scale(x1)).astype(BF)
    h2_ref[...] = dot(h2, nat_ref[...]).astype(BF)
    h2x_ref[:, :HALF] = dot(h2, pm_ref[...]).astype(BF)
    h2x_ref[:, HALF:] = dot(h2, po_ref[...]).astype(BF)
    h2z_ref[...] = dot(h2, ring_ref[...]).astype(BF)


def split(v):
    high = v.astype(BF)
    return high, (v - high.astype(F32)).astype(BF)


def backward_out(dh_ref, x1_ref, e_ref, nat_ref, om_ref, oo_ref, pm_ref, po_ref, dx1_ref, da_ref, do_ref):
    high, low = split(dh_ref[...])
    dn = dot_nt(high, nat_ref[...]) + dot_nt(low, nat_ref[...])
    x1 = x1_ref[...]
    s2 = rms_scale(x1)
    dx1 = e_ref[...].astype(F32) + s2 * dn - x1 * (s2 * s2 * s2) * jnp.mean(dn * x1, axis=-1, keepdims=True)
    dx1_ref[...] = dx1
    da = dx1.astype(BF)
    da_ref[...] = da
    dm = dot_nt(da, om_ref[...]).astype(BF)
    dt = dot_nt(da, oo_ref[...]).astype(BF)
    do_ref[...] = (dot_nt(dm, pm_ref[...]) + dot_nt(dt, po_ref[...])).astype(BF)


def input_grad(dqkv_ref, qm_ref, qo_ref, pm_ref, po_ref, dx1_ref, x_ref, w1_ref, w2_ref, w3_ref, w4_ref, w5_ref, out_ref):
    del w1_ref, w2_ref, w3_ref, w4_ref, w5_ref
    dn = jnp.zeros(dx1_ref.shape, F32)
    for w_ref, p_ref in ((qm_ref, pm_ref), (qo_ref, po_ref)):
        for part in split(dot_nt(dqkv_ref[...], w_ref[...])):
            dn += dot_nt(part, p_ref[...])
    x = x_ref[...].astype(F32)
    s1 = rms_scale(x)
    mean = jnp.mean(dn * x, axis=-1, keepdims=True)
    out_ref[...] = (dx1_ref[...] + s1 * dn - x * (s1 * s1 * s1) * mean).astype(BF)


def attention_grads(h1m_ref, h1o_ref, dqkv_ref, da_ref, mm_ref, mo_ref, w1_ref, w2_ref, w3_ref, w4_ref, gm_ref, go_ref):
    del w1_ref, w2_ref, w3_ref, w4_ref
    for g_ref, h1_ref, m_ref in ((go_ref, h1o_ref, mo_ref), (gm_ref, h1m_ref, mm_ref)):
        g_ref[:, :QKV] = dot_tn(h1_ref[...], dqkv_ref[...]).astype(BF)
        g_ref[:, QKV:] = dot_tn(m_ref[...], da_ref[...]).astype(BF)


def backward_attn(do_ref, rot_ref, prob_ref, cos_ref, sin_ref, wait1_ref, wait2_ref, dqkv_ref, work_ref):
    del wait1_ref, wait2_ref
    blocks = do_ref.shape[0] // MB
    scale = HEAD_DIM ** (-0.5)
    for b in range(blocks):
        rows = slice(b * MB, (b + 1) * MB)
        for g in range(KV_HEADS):
            heads = [slice((g * SHARE + j) * HEAD_DIM, (g * SHARE + j + 1) * HEAD_DIM) for j in range(SHARE)]
            q = jnp.concatenate([rot_ref[rows, h] for h in heads], axis=0)
            do = jnp.concatenate([do_ref[rows, h] for h in heads], axis=0)
            k = rot_ref[rows, D + g * HEAD_DIM : D + (g + 1) * HEAD_DIM]
            v = rot_ref[rows, ROT + g * HEAD_DIM : ROT + (g + 1) * HEAD_DIM]
            at = (b * KV_HEADS + g) * SHARE * MB
            p = prob_ref[at : at + SHARE * MB, :]
            dp = dot_nt(do, v)
            dv = dot_tn(p.astype(BF), do)
            delta = jnp.sum(p * dp, axis=-1, keepdims=True)
            ds = (p * (dp - delta)).astype(BF)
            dq = dot(ds, k) * scale
            dk = dot_tn(ds, q) * scale
            for j in range(SHARE):
                work_ref[:, heads[j]] = dq[j * MB : (j + 1) * MB, :]
            work_ref[:, D + g * HEAD_DIM : D + (g + 1) * HEAD_DIM] = dk
            dqkv_ref[rows, ROT + g * HEAD_DIM : ROT + (g + 1) * HEAD_DIM] = dv.astype(BF)
        cos = jnp.concatenate([cos_ref[rows, :]] * (ROT // 128), axis=1)
        sin = jnp.concatenate([sin_ref[rows, :]] * (ROT // 128), axis=1)
        w = work_ref[...]
        dqkv_ref[rows, :ROT] = (w * cos - swap_halves(w) * sin).astype(BF)


def rope_tables(segment):
    n = segment.shape[0]
    seg = segment.reshape(n // MB, MB)
    index = lax.broadcasted_iota(jnp.int32, (n // MB, MB, MB), 2)
    same = seg[:, :, None] == seg[:, None, :]
    first = jnp.min(jnp.where(same, index, MB), axis=2)
    place = (jnp.arange(MB, dtype=jnp.int32)[None, :] - first).astype(F32).reshape(n, 1)
    lane = jnp.arange(128, dtype=jnp.int32)
    freq = jnp.exp((lane % 32).astype(F32) * (-2.0 * math.log(ROPE_BASE) / HEAD_DIM))
    angles = place * freq[None, :]
    sign = jnp.where(lane % 64 < 32, -1.0, 1.0)[None, :]
    return jnp.cos(angles), jnp.sin(angles) * sign


def padding_matrix(x, z, c, first="x"):
    i = lax.broadcasted_iota(jnp.int32, (D, HALF), 0)
    j = lax.broadcasted_iota(jnp.int32, (D, HALF), 1)
    slow, fast = j // (4 * PAD), j // PAD % 4
    j_x = (x + (slow if first == "x" else fast)) % NX
    j_z = (z + (fast if first == "x" else slow)) % NZ
    j_r = j % PAD
    row = ((j_x * NZ + j_z) * 2 + c) * ROWS + j_r
    return ((i == row) & (j_r < ROWS)).astype(BF)


def natural_matrix():
    i = lax.broadcasted_iota(jnp.int32, (D, DP), 0)
    j = lax.broadcasted_iota(jnp.int32, (D, DP), 1)
    return ((i // ROWS) * PAD + i % ROWS == j).astype(BF)


def vmem_call(kernel, out_shape, scratch=(), waits=0, count=0, smem=0):
    extra = {}
    if smem:
        extra["in_specs"] = [pl.BlockSpec(memory_space=pltpu.SMEM)] + [pl.BlockSpec(memory_space=pltpu.VMEM)] * 13
    if waits:
        inside = [pl.BlockSpec(memory_space=pltpu.VMEM)] * count
        extra["in_specs"] = inside + [pl.BlockSpec(memory_space=pl.ANY)] * waits
    return pl.pallas_call(
        kernel,
        out_shape=out_shape,
        scratch_shapes=list(scratch),
        compiler_params=pltpu.CompilerParams(vmem_limit_bytes=48 * 1024 * 1024),
        cost_estimate=pl.CostEstimate(flops=1, bytes_accessed=1, transcendentals=0),
        **extra,
    )


def pass_on(v_ref, *refs):
    del v_ref, refs


def after(v, *waits):
    return pl.pallas_call(
        pass_on,
        out_shape=jax.ShapeDtypeStruct(v.shape, v.dtype),
        in_specs=[pl.BlockSpec(memory_space=pl.ANY)] * (1 + len(waits)),
        out_specs=pl.BlockSpec(memory_space=pl.ANY),
        input_output_aliases={0: 0},
        cost_estimate=pl.CostEstimate(flops=1, bytes_accessed=1, transcendentals=0),
    )(v, *waits)


def add_terms(*refs):
    for j in range(2):
        gm_ref, gg_ref, dm_ref, dg_ref = refs[4 * j : 4 * j + 4]
        out_ref = refs[len(refs) - 2 + j]
        out_ref[0, :, :PAD, :] = (gm_ref[0].astype(F32) + gg_ref[0].astype(F32)).astype(BF)
        out_ref[0, :, PAD:, :] = (dm_ref[0].astype(F32) + dg_ref[0].astype(F32)).astype(BF)


def add_terms_call(ring_x, ring_z, first, count, *waits):
    arrays = [v for ring in (ring_x, ring_z) for part in ring.parts for v in part]
    return pl.pallas_call(
        add_terms,
        grid=(count,),
        out_shape=[jax.ShapeDtypeStruct((count, 4, PAD + 16, FF), BF)] * 2,
        in_specs=[pl.BlockSpec((1,) + v.shape[1:], lambda i: (first + 2 * i, 0, 0, 0)) for v in arrays]
        + [pl.BlockSpec(memory_space=pl.ANY)] * len(waits),
        out_specs=[pl.BlockSpec((1, 4, PAD + 16, FF), lambda i: (i, 0, 0, 0))] * 2,
        compiler_params=pltpu.CompilerParams(vmem_limit_bytes=48 * 1024 * 1024),
        cost_estimate=pl.CostEstimate(flops=1, bytes_accessed=1, transcendentals=0),
    )(*arrays, *waits)


def place_of(x, z, c):
    return (x * NZ + z) * 2 + c


def shift(v, axis, s):
    if axis == "y":
        return lax.ppermute(v, "outer", [(i, (i + s) % 4) for i in range(4)])
    perm = []
    for x in range(NX):
        for z in range(NZ):
            for c in range(2):
                to = {
                    "x": ((x + s) % NX, z, c),
                    "z": (x, (z + s) % NZ, c),
                    "c": (x, z, 1 - c),
                }[axis]
                perm.append((place_of(x, z, c), place_of(*to)))
    return lax.ppermute(v, "dp", perm)


def ring_gather(s, axis, cut=None, waits=()):
    a = shift(s, axis, 1)
    b = shift(s, axis, -1)
    if cut is None:
        far = shift(s, axis, 2)
    else:
        if waits:
            a = after(a, *waits)
        far = jnp.concatenate([shift(a[:cut], axis, 1), shift(b[cut:], axis, -1)], axis=0)
    return [s, b, far, a]


def gather_attention(quarters, y, waits):
    own = lax.dynamic_index_in_dim(quarters, y, 0, keepdims=False)
    one = jnp.stack(ring_gather(own, "x"), axis=0)
    two = jnp.stack(ring_gather(one, "z", 2), axis=1).reshape(HALF, QUARTER)
    mine = jnp.stack(ring_gather(two, "y", HALF // 2, waits), axis=0)
    return mine, shift(mine, "c", 1)


def add_all(parts):
    total = parts[0].astype(F32)
    for p in parts[1:]:
        total = total + p.astype(F32)
    return total


def ring_sum(terms, axis):
    parts = [terms[0], shift(terms[2], axis, 2), shift(terms[1], axis, 1), shift(terms[3], axis, -1)]
    return add_all(parts).astype(BF)


class Ring:
    def __init__(self, pairs, first):
        self.first = first
        self.parts = []
        for mine, other in pairs:
            n = mine.shape[-1]
            rows = mine.size // (16 * n)
            got = shift(other, "c", 1).reshape(4, 4, rows, n)
            self.parts.append((mine.reshape(4, 4, rows, n), got))

    def term(self, k):
        sums = [(mine[k].astype(F32) + got[k].astype(F32)).astype(BF) for mine, got in self.parts]
        return sums[0] if len(sums) == 1 else jnp.concatenate(sums, axis=1)

    def begin(self, two=None):
        self.two = self.term(2) if two is None else two
        self.a = shift(self.two[:2], self.first, 1)
        self.b = shift(self.two[2:], self.first, -1)

    def middle(self, one=None, three=None):
        one = self.term(1) if one is None else one
        three = self.term(3) if three is None else three
        self.one = jnp.concatenate([one[:2] + self.a, one[2:]], axis=0)
        self.three = jnp.concatenate([three[:2], three[2:] + self.b], axis=0)
        self.c = shift(self.one, self.first, 1)
        self.d = shift(self.three, self.first, -1)

    def finish(self, own, *waits):
        c = after(self.c, *waits) if waits else self.c
        self.half = add_all([own, c, self.d]).astype(BF)

    def second(self):
        self.piece = ring_sum([self.half[k] for k in range(4)], "z" if self.first == "x" else "x")


def sum_outer(h, turn):
    pairs = [[(0, 1), (1, 0), (2, 3), (3, 2)], [(0, 3), (3, 0), (1, 2), (2, 1)]]
    h = h + lax.ppermute(h, "outer", pairs[turn])
    return add_all([h, lax.ppermute(h, "outer", pairs[1 - turn])])


def mlp(pos, h2_ref, h2x_ref, h2z_ref, e_ref, x1_ref, live_ref, gu_ref, down_ref,
        out_ref, gxm_ref, gxo_ref, gzm_ref, gzo_ref, dxm_ref, dxo_ref, dzm_ref, dzo_ref, dh_ref,
        acc_ref, w_ref, g_ref, hx_ref, hz_ref):
    step = pl.program_id(0)
    z, c = pos[1], pos[2]
    tile = FF // NX

    @pl.when(step == 0)
    def _():
        hx_ref[...] = h2x_ref[...].T
        hz_ref[...] = h2z_ref[...].T

    for p in range(2 * NZ):
        for b in range(DOWN // 16):
            w_ref[p * DOWN + 16 * b : p * DOWN + 16 * b + 16, :] = down_ref[p, :, 1024 * b : 1024 * b + D]
    h2 = h2_ref[...]
    e = e_ref[...]
    wgu = gu_ref[...].reshape(DP, 2 * tile)
    both = dot(h2, wgu)
    gate, up = both[:, :tile], both[:, tile:]
    sig = jax.nn.sigmoid(gate)
    silu = gate * sig
    hidden = (silu * up).astype(BF)
    d_hidden = dot_nt(e, w_ref[...])
    d_gate = (d_hidden * up * sig * (1.0 + gate * (1.0 - sig))).astype(BF)
    d_up = (d_hidden * silu).astype(BF)
    g_ref[...] = dot_tn(hidden, e)
    blank = jnp.zeros((16, 1024 - D), BF)
    for kz in range(NZ):
        at = lax.rem(z + kz, NZ) * (2 * DOWN)
        for core, dx, dz in ((c, dxm_ref.at[0, kz], dzm_ref.at[kz, 0]), (1 - c, dxo_ref.at[0, kz], dzo_ref.at[kz, 0])):
            rows = [
                g_ref[pl.ds(pl.multiple_of(at + core * DOWN + 16 * b, 16), 16), :].astype(BF)
                for b in range(DOWN // 16)
            ]
            dx[:, :D] = rows[0]
            dx[:, D:1024] = blank
            dx[:, 1024 : 1024 + D] = rows[1]
            dx[:, 1024 + D : 2048] = blank
            dx[:, 2048:] = rows[2][:, :512]
            dz[:, : D - 512] = rows[2][:, 512:]
            dz[:, D - 512 : 512] = blank
            dz[:, 512 : 512 + D] = rows[3]
            dz[:, 512 + D : 1536] = blank
            dz[:, 1536 : 1536 + D] = rows[4]
            dz[:, 1536 + D :] = blank
    gxm_ref[...] = dot(hx_ref[:HALF, :], d_gate).astype(BF)
    gxo_ref[...] = dot(hx_ref[HALF:, :], d_gate).astype(BF)
    gzm_ref[...] = dot(hz_ref[:HALF, :], d_up).astype(BF)
    gzo_ref[...] = dot(hz_ref[HALF:, :], d_up).astype(BF)
    dh = dot_nt(jnp.concatenate([d_gate, d_up], axis=1), wgu)
    y = dot(hidden, w_ref[...])

    @pl.when(step == 0)
    def _():
        dh_ref[...] = dh
        acc_ref[...] = x1_ref[...] + y

    @pl.when(step > 0)
    def _():
        dh_ref[...] += dh
        acc_ref[...] += y

    @pl.when(step == NX - 1)
    def _():
        out_ref[...] = (acc_ref[...] * live_ref[...]).astype(BF)


def mlp_call(pos, h2, h2x, h2z, e, x1, live, packed):
    n = h2.shape[0]
    tile = FF // NX

    def whole(a):
        return pl.BlockSpec(a.shape, lambda k, pos: (0,) * a.ndim)

    def here(k, pos):
        return lax.rem(pos[0] + k, NX)

    cols = pl.BlockSpec((HALF, tile), lambda k, pos: (0, here(k, pos)))
    along_x = pl.BlockSpec((1, NZ, 16, FF), lambda k, pos: (k, 0, 0, 0))
    along_z = pl.BlockSpec((NZ, 1, 16, FF), lambda k, pos: (0, k, 0, 0))
    return pl.pallas_call(
        mlp,
        out_shape=(
            jax.ShapeDtypeStruct((n, D), BF),
            *[jax.ShapeDtypeStruct((HALF, FF), BF)] * 4,
            *[jax.ShapeDtypeStruct((4, 4, 16, FF), BF)] * 4,
            jax.ShapeDtypeStruct((n, DP), F32),
        ),
        grid_spec=pltpu.PrefetchScalarGridSpec(
            num_scalar_prefetch=1,
            grid=(NX,),
            in_specs=[
                whole(h2),
                whole(h2x),
                whole(h2z),
                whole(e),
                whole(x1),
                whole(live),
                pl.BlockSpec((PIECES, PAD, 2 * tile), lambda k, pos: (0, 0, here(k, pos))),
                pl.BlockSpec((2 * NZ, 16, 2 * FF), lambda k, pos: (here(k, pos), 2, 0)),
            ],
            out_specs=(
                pl.BlockSpec((n, D), lambda k, pos: (0, 0)),
                *[cols] * 4,
                *[along_x] * 2,
                *[along_z] * 2,
                pl.BlockSpec((n, DP), lambda k, pos: (0, 0)),
            ),
            scratch_shapes=[
                pltpu.VMEM((n, D), F32),
                pltpu.VMEM((tile, D), BF),
                pltpu.VMEM((tile, D), F32),
                pltpu.VMEM((DP, n), BF),
                pltpu.VMEM((DP, n), BF),
            ],
        ),
        compiler_params=pltpu.CompilerParams(
            vmem_limit_bytes=56 * 1024 * 1024, dimension_semantics=("arbitrary",)
        ),
        cost_estimate=pl.CostEstimate(flops=1, bytes_accessed=1, transcendentals=0),
    )(pos, h2, h2x, h2z, e, x1, live, packed, packed)


def fetch(sources, targets, sem):
    copies = [pltpu.make_async_copy(a, b, sem.at[i]) for i, (a, b) in enumerate(zip(sources, targets))]
    for c in copies:
        c.start()
    for c in copies:
        c.wait()


def pack(gains_ref, *refs):
    att_ref, packed_ref = refs[7:9]
    fetch(refs[:7], refs[9:16], refs[16])
    wq_ref, wk_ref, wv_ref, wo_ref, wg_ref, wu_ref, wd_ref = refs[9:16]
    tile = FF // NX

    def padded(v):
        return jnp.concatenate([v, jnp.zeros((PAD - ROWS, v.shape[1]), F32)], axis=0).astype(BF)

    gi, gm = gains_ref[:, 0:1], gains_ref[:, 1:2]
    qkv = jnp.concatenate([wq_ref[...], wk_ref[...], wv_ref[...]], axis=1).astype(F32)
    qkv = padded(qkv * gi)
    out = padded(wo_ref[...].astype(F32))
    att_ref[0] = qkv[:, :QUARTER]
    att_ref[1] = qkv[:, QUARTER:ROT]
    att_ref[2] = jnp.concatenate([qkv[:, ROT:], out[:, QUARTER:]], axis=1)
    att_ref[3] = out[:, :QUARTER]
    for k in range(NX):
        for j, w_ref in enumerate((wg_ref, wu_ref)):
            at = (2 * k + j) * tile
            packed_ref[:PAD, at : at + tile] = padded(w_ref[:, k * tile : (k + 1) * tile].astype(F32) * gm)
    for b in range(DOWN // 16):
        rows = wd_ref[16 * b : 16 * b + 16, :]
        packed_ref[PAD:, 1024 * b : 1024 * (b + 1)] = jnp.concatenate([rows, jnp.zeros((16, 1024 - D), BF)], axis=1)


def local(
    tokens_in,
    segment_ids,
    norm_in,
    w_query,
    w_key,
    w_value,
    w_out,
    norm_mid,
    w_gate,
    w_up,
    w_down,
    out_cotangent,
):
    n = tokens_in.shape[0]
    me = lax.axis_index("dp")
    c_at = me % 2
    z_at = (me // 2) % NZ
    x_at = me // (2 * NZ)
    pos = jnp.stack([x_at, z_at, c_at]).astype(jnp.int32)
    s_qkv = jnp.concatenate([w_query, w_key, w_value], axis=1).astype(F32)
    shards = (w_query, w_key, w_value, w_out, w_gate, w_up, w_down)
    gains = jnp.stack([norm_in, norm_mid], axis=1).astype(F32)
    quarters, packed = pl.pallas_call(
        pack,
        out_shape=(
            jax.ShapeDtypeStruct((4, PAD, QUARTER), BF),
            jax.ShapeDtypeStruct((PAD + 16, 2 * FF), BF),
        ),
        in_specs=[pl.BlockSpec(memory_space=pltpu.VMEM)] + [pl.BlockSpec(memory_space=pl.ANY)] * 7,
        scratch_shapes=[pltpu.VMEM(w.shape, BF) for w in shards] + [pltpu.SemaphoreType.DMA((7,))],
        compiler_params=pltpu.CompilerParams(vmem_limit_bytes=63 * 1024 * 1024),
        cost_estimate=pl.CostEstimate(flops=1, bytes_accessed=1, transcendentals=0),
    )(gains, *shards)
    packed = lax.all_gather(packed, "dp", axis=0, tiled=False)
    y_at = lax.axis_index("outer").astype(jnp.int32)
    pad_m = padding_matrix(x_at, z_at, c_at)
    pad_o = padding_matrix(x_at, z_at, 1 - c_at)
    natural = natural_matrix()
    ring = jnp.concatenate(
        [padding_matrix(x_at, z_at, c_at, "z"), padding_matrix(x_at, z_at, 1 - c_at, "z")], axis=1
    )
    cos, sin = rope_tables(segment_ids)
    live = (segment_ids < DOCS).astype(F32)[:, None]
    e_low = (out_cotangent.astype(F32) * live).astype(BF)
    x = tokens_in.astype(F32)
    s1 = rms_scale(x)
    h1 = (x * s1).astype(BF)
    h1_m, h1_o = dot(h1, pad_m).astype(BF), dot(h1, pad_o).astype(BF)
    att_m, att_o = gather_attention(quarters, y_at, (natural, ring, h1_m, h1_o, cos, sin, e_low))
    rot, probs, mixed_m, mixed_o, x1, h2, h2x, h2z, qkv_m, qkv_o, out_m, out_o = vmem_call(
        forward,
        (
            jax.ShapeDtypeStruct((n, QKV), BF),
            jax.ShapeDtypeStruct((n * HEADS, MB), F32),
            jax.ShapeDtypeStruct((n, HALF), BF),
            jax.ShapeDtypeStruct((n, HALF), BF),
            jax.ShapeDtypeStruct((n, D), F32),
            jax.ShapeDtypeStruct((n, DP), BF),
            jax.ShapeDtypeStruct((n, DP), BF),
            jax.ShapeDtypeStruct((n, DP), BF),
            jax.ShapeDtypeStruct((HALF, QKV), BF),
            jax.ShapeDtypeStruct((HALF, QKV), BF),
            jax.ShapeDtypeStruct((HALF, D), BF),
            jax.ShapeDtypeStruct((HALF, D), BF),
        ),
        [pltpu.VMEM((n, QKV), F32), pltpu.VMEM((n, D), BF)],
            smem=1,
    )(y_at[None], h1_m, h1_o, att_m, att_o, cos, sin, segment_ids[:, None], segment_ids.reshape(n // MB, MB),
      tokens_in, pad_m, pad_o, natural, ring)

    layer_out, gx_m, gx_o, gz_m, gz_o, dx_m, dx_o, dz_m, dz_o, dh2 = mlp_call(
        pos, h2, h2x, h2z, e_low, x1, live, packed
    )
    ring_x = Ring([(gx_m, gx_o), (dx_m, dx_o)], "x")
    ring_z = Ring([(gz_m, gz_o), (dz_m, dz_o)], "z")
    two_x, two_z = add_terms_call(ring_x, ring_z, 2, 1)
    ring_x.begin(two_x[0])
    ring_z.begin(two_z[0])
    d_x1, d_a, d_o = vmem_call(
        backward_out,
        (
            jax.ShapeDtypeStruct((n, D), F32),
            jax.ShapeDtypeStruct((n, D), BF),
            jax.ShapeDtypeStruct((n, D), BF),
        ),
    )(dh2, x1, e_low, natural, out_m, out_o, pad_m, pad_o)
    d_qkv = vmem_call(
        backward_attn,
        jax.ShapeDtypeStruct((n, QKV), BF),
        [pltpu.VMEM((MB, ROT), F32)],
        waits=2,
        count=5,
    )(d_o, rot, probs, cos, sin, ring_x.two, ring_z.two)
    ga_m, ga_o = vmem_call(
        attention_grads,
        (jax.ShapeDtypeStruct((HALF, QKV + D), BF), jax.ShapeDtypeStruct((HALF, QKV + D), BF)),
        waits=4,
        count=6,
    )(h1_m, h1_o, d_qkv, d_a, mixed_m, mixed_o, ring_x.a, ring_x.b, ring_z.a, ring_z.b)
    rest_x, rest_z = add_terms_call(ring_x, ring_z, 1, 2, d_qkv)
    ring_att = Ring([(ga_m, ga_o)], "x")
    ring_x.middle(rest_x[0], rest_x[1])
    ring_z.middle(rest_z[0], rest_z[1])
    ring_att.begin()
    grad_input = vmem_call(
        input_grad, jax.ShapeDtypeStruct((n, D), BF), waits=5, count=7
    )(d_qkv, qkv_m, qkv_o, pad_m, pad_o, d_x1, tokens_in, ring_x.one, ring_x.three, ring_z.one, ring_z.three, ring_att.two)
    ring_x.finish(ring_x.term(0), grad_input, ring_att.a)
    ring_z.finish(ring_z.term(0), grad_input, ring_att.b)
    layer_out = after(layer_out, grad_input)
    ring_att.middle()
    ring_att.finish(ring_att.term(0))
    ring_x.second()
    ring_z.second()
    ring_att.second()
    gd_x = sum_outer(after(ring_x.piece, ring_att.one), 0)
    gd_z = sum_outer(after(ring_z.piece, ring_att.one), 1)
    g_att = sum_outer(ring_att.piece, 0)[:ROWS]
    g_gate, g_up = gd_x[:ROWS], gd_z[:ROWS]
    gd_x, gd_z = gd_x[PAD:], gd_z[PAD:]
    g_down = jnp.concatenate(
        [
            gd_x[:, :D],
            gd_x[:, 1024 : 1024 + D],
            jnp.concatenate([gd_x[:, 2048:], gd_z[:, : D - 512]], axis=1),
            gd_z[:, 512 : 512 + D],
            gd_z[:, 1536 : 1536 + D],
        ],
        axis=0,
    )
    g_qkv, g_out = g_att[:, :QKV], g_att[:, QKV:]

    gain_in, gain_mid = gains[:, 0:1], gains[:, 1:2]
    g_norm_in = jnp.sum(g_qkv * s_qkv, axis=1)
    g_norm_mid = jnp.sum(g_gate * w_gate.astype(F32) + g_up * w_up.astype(F32), axis=1)
    g_qkv = g_qkv * gain_in
    return (
        layer_out,
        grad_input,
        g_norm_in,
        g_qkv[:, :D],
        g_qkv[:, D:ROT],
        g_qkv[:, ROT:],
        g_out,
        g_norm_mid,
        g_gate * gain_mid,
        g_up * gain_mid,
        g_down,
    )


def solution(mesh):
    rows = P(("dp", "outer"), None)
    ids = P(("dp", "outer"))
    vec = P("dp")
    mat = P("dp", None)
    in_specs = (rows, ids, vec, mat, mat, mat, mat, vec, mat, mat, mat, rows)
    out_specs = (rows, rows, vec, mat, mat, mat, mat, vec, mat, mat, mat)
    return jax.shard_map(local, mesh=mesh, in_specs=in_specs, out_specs=out_specs, check_vma=False)
```
